128 devices in a mesh: row: 8 (over y_lo, z), col: 8 (over x, y_hi), depth: 2 (over core).
Axes of the slice: x: 4, y: 4 (y_hi: 2, y_lo: 2; y = y_hi * 2 + y_lo), z: 4, core: 2. Of those that a mesh axis runs over, the one named last changes fastest.
Arguments:
- quant_codes: int32 [12288, 6144], P(('row', 'depth'), 'col'), may hold values from 0 to 15
- block_scales: float32 [96, 12288], P('col', ('row', 'depth')), may hold values from 0.14 to 0.3
Outputs:
- rectified: bfloat16 [12288, 6144], P(('row', 'depth'), 'col')
- gram_matrix: bfloat16 [6144, 6144], P(('row', 'depth'), 'col')
The draws below stay inside these ranges and needn't reach their ends.
All inputs are finite; a program needn't handle non-finite values.
Results may differ from the reference program's by a relative error of at most 0.0059.
Values may be sent and summed in bfloat16 or wider, within the bound.
No kernel may reach another device: no remote copies, remote signals or barrier semaphores. Data moves between devices by JAX's collectives and lax.ppermute only.
A program may use at most 128 MiB of HBM per device.

```python
import math
import jax
import jax.numpy as jnp
from jax import lax

N = 12288
BLOCK = 64
K = 6144


def touch_ends(array, rng, least, largest):
    longest = array.shape.index(max(array.shape))
    spots = []
    for shift in (0, 1):
        where = [jax.random.randint(jax.random.fold_in(rng, axis), (), 0, length) for axis, length in enumerate(array.shape)]
        where[longest] = (where[longest] + shift) % array.shape[longest]
        spots.append(tuple(where))
    return array.at[spots[0]].set(least).at[spots[1]].set(largest)


def shard_levels(rng, shape, cuts, low, largest):
    factor_of, own = 1.0, jax.random.fold_in(rng, 6)
    for position, blocks in cuts:
        steps = jnp.exp(jax.random.uniform(jax.random.fold_in(own, position), (blocks,), jnp.float32, low / len(cuts), largest / len(cuts)))
        factor_of = factor_of * jnp.repeat(steps, shape[position] // blocks).reshape([-1 if axis == position else 1 for axis in range(len(shape))])
    return factor_of


def setup_inputs(seed: int = 0) -> dict:
    seeds = jax.random.split(jax.random.key(seed), 3)
    quant_codes = touch_ends(jax.random.randint(seeds[0], (N, K), 0, 16), jax.random.fold_in(seeds[0], 1), 0, 15).astype(jnp.int32)
    block_scales = jnp.clip(jnp.exp(math.log(0.3) - 0.7621401 * jax.random.uniform(seeds[1], (K // BLOCK, N), jnp.float32) ** shard_levels(seeds[1], (K // BLOCK, N), ((0, 8), (1, 16)), -0.2, 0.2)), 0.14, 0.3)
    return {"quant_codes": quant_codes, "block_scales": block_scales}


def dequantize(quant_codes, block_scales):
    row_count, col_count = quant_codes.shape
    levels = quant_codes.astype(jnp.float32).reshape(row_count, col_count // BLOCK, BLOCK) - 7.5
    factor = jnp.transpose(block_scales)
    return (levels * factor[:, :, None]).reshape(row_count, col_count).astype(jnp.bfloat16)


def reference(quant_codes, block_scales):
    basis_full = dequantize(quant_codes, block_scales)
    widened = basis_full.astype(jnp.float32)
    gram_sum = jnp.dot(widened.T, widened, precision=lax.Precision.HIGHEST)
    gram_matrix = (gram_sum * (1.0 / N)).astype(jnp.bfloat16)
    product = jnp.dot(widened, gram_matrix.astype(jnp.float32), precision=lax.Precision.HIGHEST)
    rectified = (1.5 * widened - 0.5 * product).astype(jnp.bfloat16)
    return rectified, gram_matrix
```

```python
import jax
import jax.numpy as jnp
from jax import lax
from jax.sharding import Mesh, PartitionSpec as P

N = 12288
BLOCK = 64
AXES = ("yl", "z", "x", "yh", "core")
F32, BF16 = jnp.float32, jnp.bfloat16


def ring(axis, step):
    return lambda a: lax.ppermute(a, axis, [(i, (i + step) % 4) for i in range(4)])


def swap(axis):
    return lambda a: lax.ppermute(a, axis, [(0, 1), (1, 0)])


def tdot(a, b):
    return lax.dot_general(a, b, (((0,), (0,)), ((), ())), preferred_element_type=F32)


def dot(a, b):
    return jnp.dot(a, b, preferred_element_type=F32)


def dot_t(a, b):
    return lax.dot_general(a, b, (((1,), (1,)), ((), ())), preferred_element_type=F32)


def pick(a, i):
    return lax.dynamic_index_in_dim(a, i, 0, keepdims=False)


def body(quant_codes, block_scales):
    yl, z, x, h, k = (lax.axis_index(a) for a in AXES)
    rows, cols = quant_codes.shape
    half = cols // 2
    levels = quant_codes.astype(F32).reshape(rows, cols // BLOCK, BLOCK) - 7.5
    factor = jnp.transpose(block_scales)
    own = (levels * factor[:, :, None]).reshape(rows, cols).astype(BF16)

    near1 = ring("x", -1)(own)
    near3 = ring("x", 1)(own)
    far = swap("yh")(own)
    near2 = jnp.concatenate([ring("x", -1)(near1[: rows // 2]), ring("x", 1)(near3[rows // 2 :])])
    later, _ = lax.optimization_barrier((far, near2))
    far1 = ring("x", -1)(later)
    far3 = ring("x", 1)(later)
    far2 = jnp.concatenate([ring("x", -1)(far1[: rows // 2]), ring("x", 1)(far3[rows // 2 :])])

    low = x < 2

    def half_tile(upper, lower, first):
        return jnp.where(first, upper[:, :half], upper[:, half:]), lower

    def reduce(parts):
        pieces = [p.astype(BF16).reshape(2, 4, p.shape[0] // 8, cols) for p in parts]
        wide = jnp.concatenate(pieces, axis=2) if len(pieces) > 1 else pieces[0]
        other = swap("core")(pick(wide, 1 - k))
        mine = pick(wide, k)

        def slab(j):
            i = (z + j) % 4
            return pick(mine, i).astype(F32) + pick(other, i).astype(F32)

        total = slab(0)
        got = [ring("z", j)(slab(j).astype(BF16)) for j in (1, 3, 2)]
        for g in got:
            total = total + g.astype(F32)
        total = total.astype(BF16)
        total = total.astype(F32) + swap("yl")(total).astype(F32)
        return (total * (1.0 / N)).astype(BF16)

    def spread(shard):
        got = [shard] + [ring("z", -j)(shard) for j in (1, 2, 3)]
        buf = jnp.zeros((4,) + shard.shape, BF16)
        for j, g in enumerate(got):
            buf = lax.dynamic_update_slice(buf, g[None], ((z + j) % 4, 0, 0))
        other = swap("core")(buf)
        return jnp.where(k == 0, buf, other), jnp.where(k == 0, other, buf)

    def tile(both, at, size):
        return jnp.concatenate([b[:, at : at + size].reshape(4 * size, cols) for b in both])

    both0 = spread(reduce([tdot(own, own)]))
    g00 = tile(both0, 0, 96)
    lhs, rhs = half_tile(jnp.where(h == 0, far, own), jnp.where(h == 0, own, far), h == 0)
    shard = reduce([tdot(near1, own), tdot(near1, far), tdot(lhs, rhs)])
    sh01 = shard[192:240]
    from_x = ring("x", 1)(shard[:192])
    from_y = swap("yh")(shard[96:240])
    sh01_both = [jnp.where(h == 0, sh01, from_y[96:]), jnp.where(h == 0, from_y[96:], sh01)]
    both1 = spread(jnp.concatenate([shard[:96], from_x, from_y[:96]] + sh01_both))
    g10 = tile(both1, 0, 96)
    g30 = tile(both1, 96, 96)
    g31 = tile(both1, 192, 96)
    g11 = tile(both1, 288, 96)
    g01 = jnp.concatenate([tile(both1, 384, 48), tile(both1, 432, 48)])
    lhs0, rhs0 = half_tile(jnp.where(low, near2, own), jnp.where(low, own, near2), low)
    lhs1, rhs1 = half_tile(jnp.where(low, near2, far), jnp.where(low, far, near2), low)
    shard = reduce([tdot(lhs0, rhs0), tdot(lhs1, rhs1)])
    from_x = ring("x", 2)(shard)
    from_y = swap("yh")(shard[48:])
    first = [jnp.where(low, shard[:48], from_x[:48]), jnp.where(low, from_x[:48], shard[:48])]
    second = [jnp.where(low, from_y, from_x[48:]), jnp.where(low, from_x[48:], from_y)]
    both2 = spread(jnp.concatenate(first + second))
    g20 = jnp.concatenate([tile(both2, 0, 48), tile(both2, 48, 48)])
    g21 = jnp.concatenate([tile(both2, 96, 48), tile(both2, 144, 48)])

    g01 = jnp.where(h == 0, g01, g01.T)
    g20 = jnp.where(low, g20, g20.T)
    g21 = jnp.where(low, g21, g21.T)
    product = (
        dot(own, g00) + dot(near1, g10) + dot_t(near3, g30) + dot(far1, g11) + dot_t(far3, g31)
        + dot(far, g01) + dot(near2, g20) + dot(far2, g21)
    )
    rectified = (1.5 * own.astype(F32) - 0.5 * product).astype(BF16)

    def straight(g):
        return lambda: lax.dynamic_slice(g, (k * half, 0), (half, cols))

    def turned(g):
        return lambda: lax.dynamic_slice(g, (0, k * half), (cols, half)).T

    line = yl * 4 + z
    which = 2 * ((line // 2 - x) % 4) + (line % 2 + h) % 2
    gram = lax.switch(
        which,
        [straight(g00), straight(g01), straight(g10), straight(g11), straight(g20), straight(g21), turned(g30), turned(g31)],
    )
    return (rectified, gram)


def solution(mesh):
    split = Mesh(mesh.devices.reshape(2, 4, 4, 2, 2), AXES)
    line, side = ("yl", "z", "core"), ("x", "yh")
    return jax.shard_map(
        body,
        mesh=split,
        in_specs=(P(line, side), P(side, line)),
        out_specs=(P(line, side), P(line, side)),
        check_vma=False,
    )
```

```python
import functools

import jax
import jax.numpy as jnp
from jax import lax
from jax.experimental import pallas as pl
from jax.experimental.pallas import tpu as pltpu
from jax.sharding import Mesh, PartitionSpec as P

N = 12288
BLOCK = 64
AXES = ("yl", "z", "x", "yh", "core")
F32, BF16 = jnp.float32, jnp.bfloat16
T = 768
H = T // 2
S = 48
VMEM = pl.BlockSpec(memory_space=pltpu.VMEM)
ANY = pl.BlockSpec(memory_space=pl.ANY)


def ring(axis, step):
    return lambda a: lax.ppermute(a, axis, [(i, (i + step) % 4) for i in range(4)])


def swap(axis):
    return lambda a: lax.ppermute(a, axis, [(0, 1), (1, 0)])


def tdot(a, b):
    return lax.dot_general(a, b, (((0,), (0,)), ((), ())), preferred_element_type=F32)


def dot(a, b):
    return jnp.dot(a, b, preferred_element_type=F32)


def dot_t(a, b):
    return lax.dot_general(a, b, (((1,), (1,)), ((), ())), preferred_element_type=F32)


def params(mib):
    return pltpu.CompilerParams(vmem_limit_bytes=mib << 20)


def cost(flops, size):
    return pl.CostEstimate(flops=flops, bytes_accessed=size, transcendentals=0)


def dequant_kernel(codes, scales, out):
    factor = scales[...].T
    lane = lax.broadcasted_iota(jnp.int32, (T, 128), 1)
    for g in range(T // 128):
        both = jnp.where(lane < BLOCK, factor[:, 2 * g : 2 * g + 1], factor[:, 2 * g + 1 : 2 * g + 2])
        levels = codes[:, 128 * g : 128 * (g + 1)].astype(F32) - 7.5
        out[:, 128 * g : 128 * (g + 1)] = (levels * both).astype(BF16)


def dequant(codes, scales):
    return pl.pallas_call(
        dequant_kernel,
        out_shape=jax.ShapeDtypeStruct((T, T), BF16),
        in_specs=[VMEM, VMEM],
        out_specs=VMEM,
        compiler_params=params(24),
        cost_estimate=cost(2 * T * T, 6 * T * T),
    )(codes, scales)


def cut(full, first, count, keep, send):
    z, k = lax.axis_index("z"), lax.axis_index("core")
    for half in range(count):
        for j in range(4):
            at = half * H + lax.rem(z + j, 4) * S
            to = pl.ds((first + half) * S, S)
            keep[j, to, :] = full[pl.ds(pl.multiple_of(at + k * (4 * S), 16), S), :].astype(BF16)
            send[j, to, :] = full[pl.ds(pl.multiple_of(at + (1 - k) * (4 * S), 16), S), :].astype(BF16)


def gram_kernel0(own, keep, send, full):
    full[...] = tdot(own[...], own[...])
    cut(full, 0, 2, keep, send)


def gram_kernel1(own, near1, far, keep, send, full):
    turned = near1[...].T
    full[...] = dot(turned, own[...])
    cut(full, 0, 2, keep, send)
    full[...] = dot(turned, far[...])
    cut(full, 2, 2, keep, send)
    h = lax.axis_index("yh")

    @pl.when(h == 0)
    def _():
        full[0:H, :] = tdot(far[:, 0:H], own[...])

    @pl.when(h != 0)
    def _():
        full[0:H, :] = tdot(own[:, H:T], far[...])

    cut(full, 4, 1, keep, send)


def gram_kernel2(own, far, near2a, near2b, keep, send, full):
    low = lax.axis_index("x") < 2
    for i, other in enumerate((own, far)):

        @pl.when(low)
        def _():
            full[0:H, :] = tdot(near2a[:, 0:H], other[0:H, :]) + tdot(near2b[:, 0:H], other[H:T, :])

        @pl.when(jnp.logical_not(low))
        def _():
            full[0:H, :] = tdot(other[0:H, H:T], near2a[...]) + tdot(other[H:T, H:T], near2b[...])

        cut(full, i, 1, keep, send)


def gram(kernel, halves, *tiles):
    out = jax.ShapeDtypeStruct((4, halves * S, T), BF16)
    return pl.pallas_call(
        kernel,
        out_shape=(out, out),
        in_specs=[VMEM] * len(tiles),
        out_specs=(VMEM, VMEM),
        scratch_shapes=[pltpu.VMEM((T, T), F32)],
        compiler_params=params(32),
        cost_estimate=cost(halves * T * T * T, 6 * T * T),
    )(*tiles)


PIECES = (2, 10, 4)


def product_kernel(*refs):
    own, near1, near3, far3, far1, far, near2a, near2b, far2a, far2b = refs[:10]
    slices = refs[10 : 10 + 24]
    out, gram_out = refs[34:36]
    a, g, acc, a_sem, g_sem = refs[36:]
    z, k, h = lax.axis_index("z"), lax.axis_index("core"), lax.axis_index("yh")
    x, yl = lax.axis_index("x"), lax.axis_index("yl")
    low = x < 2

    a_copies = []
    for i, src in enumerate((own, near1, near3, far3, far1, far)):
        a_copies.append([pltpu.make_async_copy(src, a.at[i], a_sem.at[i])])
    for i, (top, bottom) in ((6, (near2a, near2b)), (7, (far2a, far2b))):
        a_copies.append(
            [
                pltpu.make_async_copy(top, a.at[i, pl.ds(0, H)], a_sem.at[i]),
                pltpu.make_async_copy(bottom, a.at[i, pl.ds(H, H)], a_sem.at[i + 2]),
            ]
        )
    g_copies, first = [], 0
    for p, count in enumerate(PIECES):
        piece = []
        for c in range(2):
            for j in range(4):
                src = slices[p * 8 + c * 4 + j]
                core = k if c == 0 else 1 - k
                at = pl.multiple_of(core * (4 * S) + lax.rem(z + j, 4) * S, 16)
                piece.append(
                    pltpu.make_async_copy(src, g.at[pl.ds(first, count), pl.ds(at, S)], g_sem.at[p * 8 + c * 4 + j])
                )
        g_copies.append(piece)
        first += count
    for group in a_copies + g_copies:
        for copy in group:
            copy.start()

    def tile(t):
        return g[2 * t : 2 * t + 2].reshape(T, T)

    def add(t, turn):
        for copy in a_copies[t]:
            copy.wait()
        if isinstance(turn, bool):
            acc[...] += dot_t(a[t], tile(t)) if turn else dot(a[t], tile(t))
            return

        @pl.when(turn)
        def _():
            acc[...] += dot_t(a[t], tile(t))

        @pl.when(jnp.logical_not(turn))
        def _():
            acc[...] += dot(a[t], tile(t))

    for copy in g_copies[0]:
        copy.wait()
    for copy in a_copies[0]:
        copy.wait()
    acc[...] = dot(a[0], tile(0))
    for copy in g_copies[1]:
        copy.wait()
    add(1, False)
    add(2, True)
    add(3, True)
    add(4, False)
    add(5, h != 0)
    for copy in g_copies[2]:
        copy.wait()
    add(6, x >= 2)
    add(7, x >= 2)
    out[...] = (1.5 * a[0].astype(F32) - 0.5 * acc[...]).astype(BF16)

    line = yl * 4 + z
    dx, dh = lax.rem(line // 2 - x + 4, 4), lax.rem(lax.rem(line, 2) + h, 2)
    where = ((0, 5), (1, 4), (6, 7), (2, 3))
    which = jnp.int32(0)
    for i, pair in enumerate(where):
        for j, t in enumerate(pair):
            which = jnp.where((dx == i) & (dh == j), t, which)
    turn = (which == 2) | (which == 3) | ((which == 5) & (h != 0)) | ((which >= 6) & (x >= 2))

    @pl.when(jnp.logical_not(turn))
    def _():
        gram_out[...] = g[2 * which + k]

    for side in range(2):

        @pl.when(turn & (k == side))
        def _():
            columns = g[pl.ds(2 * which, 2), :, side * H : (side + 1) * H].reshape(T, H)
            gram_out[...] = columns.T


def product(tiles, slices):
    return pl.pallas_call(
        product_kernel,
        out_shape=(jax.ShapeDtypeStruct((T, T), BF16), jax.ShapeDtypeStruct((H, T), BF16)),
        in_specs=[ANY] * (len(tiles) + len(slices)),
        out_specs=(VMEM, VMEM),
        scratch_shapes=[
            pltpu.VMEM((8, T, T), BF16),
            pltpu.VMEM((16, H, T), BF16),
            pltpu.VMEM((T, T), F32),
            pltpu.SemaphoreType.DMA((10,)),
            pltpu.SemaphoreType.DMA((24,)),
        ],
        compiler_params=params(40),
        cost_estimate=cost(16 * T * T * T, 36 * T * T),
    )(*tiles, *slices)


def reduce(keep, send):
    other = swap("core")(send)
    sums = [keep[j].astype(F32) + other[j].astype(F32) for j in range(4)]
    got = [ring("z", j)(sums[j].astype(BF16)) for j in (1, 3, 2)]
    total = sums[0]
    for piece in got:
        total = total + piece.astype(F32)
    total = total.astype(BF16)
    total = total.astype(F32) + swap("yl")(total).astype(F32)
    return (total * (1.0 / N)).astype(BF16)


def spread(*parts):
    shard = jnp.concatenate(parts).reshape(-1, S, T)
    mine = [shard] + [ring("z", -j)(shard) for j in (1, 2, 3)]
    return mine + [swap("core")(a) for a in mine]


def body(quant_codes, block_scales):
    h, low = lax.axis_index("yh"), lax.axis_index("x") < 2
    own = dequant(quant_codes, block_scales)

    near1 = ring("x", -1)(own)
    near3 = ring("x", 1)(own)
    far = swap("yh")(own)
    shard0 = reduce(*gram(gram_kernel0, 2, own))
    slices0 = spread(shard0)
    near2 = [ring("x", -1)(near1[:H]), ring("x", 1)(near3[H:])]

    keep, send = gram(gram_kernel1, 5, own, near1, far)
    shard = reduce(keep, send)
    later, _, _ = lax.optimization_barrier((far, near2[0], near2[1]))
    far1 = ring("x", -1)(later)
    far3 = ring("x", 1)(later)
    far2 = [ring("x", -1)(far1[:H]), ring("x", 1)(far3[H:])]
    mine = shard[4 * S :]
    from_x = ring("x", 1)(shard[: 4 * S])
    from_y = swap("yh")(shard[2 * S :])
    theirs = from_y[2 * S :]
    slices1 = spread(
        shard[: 2 * S], from_x, from_y[: 2 * S], jnp.where(h == 0, mine, theirs), jnp.where(h == 0, theirs, mine)
    )

    shard = reduce(*gram(gram_kernel2, 2, own, far, *near2))
    from_x = ring("x", 2)(shard)
    from_y = swap("yh")(shard[S:])
    mine, theirs = jnp.concatenate([shard[:S], from_y]), from_x
    first, second = jnp.where(low, mine, theirs), jnp.where(low, theirs, mine)
    slices2 = spread(first[:S], second[:S], first[S:], second[S:])

    return product([own, near1, near3, far3, far1, far] + near2 + far2, slices0 + slices1 + slices2)


def solution(mesh):
    split = Mesh(mesh.devices.reshape(2, 4, 4, 2, 2), AXES)
    line, side = ("yl", "z", "core"), ("x", "yh")
    return jax.shard_map(
        body,
        mesh=split,
        in_specs=(P(line, side), P(side, line)),
        out_specs=(P(line, side), P(line, side)),
        check_vma=False,
    )
```

```python
import functools

import jax
import jax.numpy as jnp
from jax import lax
from jax.experimental import pallas as pl
from jax.experimental.pallas import tpu as pltpu
from jax.sharding import Mesh, PartitionSpec as P

N = 12288
BLOCK = 64
AXES = ("yl", "z", "x", "yh", "core")
F32, BF16 = jnp.float32, jnp.bfloat16
T = 768
H = T // 2
S = 48
VMEM = pl.BlockSpec(memory_space=pltpu.VMEM)


def ring(axis, step):
    return lambda a: lax.ppermute(a, axis, [(i, (i + step) % 4) for i in range(4)])


def swap(axis):
    return lambda a: lax.ppermute(a, axis, [(0, 1), (1, 0)])


def tdot(a, b):
    return lax.dot_general(a, b, (((0,), (0,)), ((), ())), preferred_element_type=F32)


def dot(a, b):
    return jnp.dot(a, b, preferred_element_type=F32)


def dot_t(a, b):
    return lax.dot_general(a, b, (((1,), (1,)), ((), ())), preferred_element_type=F32)


def params(mib):
    return pltpu.CompilerParams(vmem_limit_bytes=mib << 20)


def cost(flops, size):
    return pl.CostEstimate(flops=flops, bytes_accessed=size, transcendentals=0)


def dequant_kernel(codes, scales, out):
    factor = scales[...].T
    lane = lax.broadcasted_iota(jnp.int32, (T, 128), 1)
    for g in range(T // 128):
        both = jnp.where(lane < BLOCK, factor[:, 2 * g : 2 * g + 1], factor[:, 2 * g + 1 : 2 * g + 2])
        levels = codes[:, 128 * g : 128 * (g + 1)].astype(F32) - 7.5
        out[:, 128 * g : 128 * (g + 1)] = (levels * both).astype(BF16)


def dequant(codes, scales):
    return pl.pallas_call(
        dequant_kernel,
        out_shape=jax.ShapeDtypeStruct((T, T), BF16),
        in_specs=[VMEM, VMEM],
        out_specs=VMEM,
        compiler_params=params(12),
        cost_estimate=cost(2 * T * T, 6 * T * T),
    )(codes, scales)


def cut(full, first, count, keep, send):
    z, k = lax.axis_index("z"), lax.axis_index("core")
    for half in range(count):
        for j in range(4):
            at = half * H + lax.rem(z + j, 4) * S
            to = pl.ds((first + half) * S, S)
            keep[j, to, :] = full[pl.ds(pl.multiple_of(at + k * (4 * S), 16), S), :].astype(BF16)
            send[j, to, :] = full[pl.ds(pl.multiple_of(at + (1 - k) * (4 * S), 16), S), :].astype(BF16)


def gram_kernel0(own, keep, send, full):
    full[...] = tdot(own[...], own[...])
    cut(full, 0, 2, keep, send)


def gram_kernel1(own, near1, far, _, keep, send, full):
    turned = near1[...].T
    full[...] = dot(turned, own[...])
    cut(full, 0, 2, keep, send)
    full[...] = dot(turned, far[...])
    cut(full, 2, 2, keep, send)
    h = lax.axis_index("yh")

    @pl.when(h == 0)
    def _():
        full[0:H, :] = tdot(far[:, 0:H], own[...])

    @pl.when(h != 0)
    def _():
        full[0:H, :] = tdot(own[:, H:T], far[...])

    cut(full, 4, 1, keep, send)


def gram_kernel2(own, far, near2a, near2b, _, keep, send, full):
    low = lax.axis_index("x") < 2
    for i, other in enumerate((own, far)):

        @pl.when(low)
        def _():
            full[0:H, :] = tdot(near2a[:, 0:H], other[0:H, :]) + tdot(near2b[:, 0:H], other[H:T, :])

        @pl.when(jnp.logical_not(low))
        def _():
            full[0:H, :] = tdot(other[0:H, H:T], near2a[...]) + tdot(other[H:T, H:T], near2b[...])

        cut(full, i, 1, keep, send)


def gram(kernel, halves, tiles, later=()):
    out = jax.ShapeDtypeStruct((4, halves * S, T), BF16)
    return pl.pallas_call(
        kernel,
        out_shape=(out, out),
        in_specs=[VMEM] * (len(tiles) + len(later)),
        out_specs=(VMEM, VMEM),
        scratch_shapes=[pltpu.VMEM((T, T), F32)],
        compiler_params=params(14),
        cost_estimate=cost(halves * T * T * T, 6 * T * T),
    )(*tiles, *later)


def halves_kernel(near1, near3, _, top, bottom):
    top[...] = near1[0:H, :]
    bottom[...] = near3[H:T, :]


def halves(near1, near3, later):
    out = jax.ShapeDtypeStruct((H, T), BF16)
    return pl.pallas_call(
        halves_kernel,
        out_shape=(out, out),
        in_specs=[VMEM, VMEM, VMEM],
        out_specs=(VMEM, VMEM),
        compiler_params=params(8),
        cost_estimate=cost(0, 4 * T * T),
    )(near1, near3, later)


def gate_kernel(*refs):
    pass


def gate(value, *later):
    return pl.pallas_call(
        gate_kernel,
        out_shape=jax.ShapeDtypeStruct(value.shape, value.dtype),
        in_specs=[VMEM] * (1 + len(later)),
        out_specs=VMEM,
        input_output_aliases={0: 0},
        compiler_params=params(8),
        cost_estimate=cost(0, 0),
    )(value, *later)


def line_kernel1(shard, from_x, from_y, _, __, out):
    out[0 : 2 * S] = shard[0 : 2 * S]
    out[2 * S : 6 * S] = from_x[...]
    out[6 * S : 8 * S] = from_y[0 : 2 * S]
    h = lax.axis_index("yh")
    out[pl.ds(pl.multiple_of((8 + h) * S, S), S)] = shard[4 * S : 5 * S]
    out[pl.ds(pl.multiple_of((9 - h) * S, S), S)] = from_y[2 * S : 3 * S]


def line_kernel2(shard, from_x, from_y, _, __, ___, ____, out):
    out[0 : 2 * S] = shard[0 : 2 * S]
    high = (lax.axis_index("x") >= 2).astype(jnp.int32)
    for at, mine, theirs in (
        (2, shard[2 * S : 3 * S], from_x[0:S]),
        (4, from_y[...], from_x[S : 2 * S]),
    ):
        out[pl.ds(pl.multiple_of((at + high) * S, S), S)] = mine
        out[pl.ds(pl.multiple_of((at + 1 - high) * S, S), S)] = theirs


def line_up(kernel, count, parts, later=()):
    return pl.pallas_call(
        kernel,
        out_shape=jax.ShapeDtypeStruct((count * S, T), BF16),
        in_specs=[VMEM] * (len(parts) + len(later)),
        out_specs=VMEM,
        compiler_params=params(8),
        cost_estimate=cost(0, 4 * count * S * T),
    )(*parts, *later).reshape(count, S, T)


def product_kernel(plan, final, *refs):
    count = len(plan)
    x, h, z, k = (lax.axis_index(axis) for axis in ("x", "yh", "z", "core"))
    refs = list(refs)
    tiles = [[refs.pop(0) for _ in source] for _, source, _ in plan]
    slices = [refs.pop(0) for _ in range(10)]
    before = [refs.pop(0) for _ in range(2 if final else 0)]
    out, gram_out, g, g_sem = refs[:4]
    acc = refs[4] if final else out

    g_copies = []
    ranges = ((0, 0, 2 * count), (1, 0, 2 * count), (3, 0, 2 * count), (2, 0, count), (2, count, count))
    for c in range(2):
        for i, (j, first, size) in enumerate(ranges):
            core = k if c == 0 else 1 - k
            at = pl.multiple_of(core * (4 * S) + lax.rem(z + j, 4) * S, 16)
            n = c * 5 + i
            g_copies.append(pltpu.make_async_copy(slices[n], g.at[pl.ds(first, size), pl.ds(at, S)], g_sem.at[n]))
    for copy in g_copies:
        copy.start()
    for copy in g_copies:
        copy.wait()

    def tile(t):
        return g[2 * t : 2 * t + 2].reshape(T, T)

    def is_turned(turn):
        return {"no": z < 0, "yes": z >= 0, "h": h != 0, "x": x >= 2}[turn]

    for t, (_, _, turn) in enumerate(plan):
        turned = is_turned(turn)

        def add(multiply):
            at = 0
            for part in tiles[t]:
                rows = slice(at, at + part.shape[0])
                value = multiply(part[...], tile(t))
                if t > 0:
                    acc[rows, :] += value
                elif final:
                    acc[rows, :] = before[0][rows, :] + value
                else:
                    acc[rows, :] = value
                at += part.shape[0]

        if turn != "yes":

            @pl.when(jnp.logical_not(turned))
            def _():
                add(dot)

        if turn != "no":

            @pl.when(turned)
            def _():
                add(dot_t)

    if final:
        out[...] = (1.5 * tiles[0][0][...].astype(F32) - 0.5 * acc[...]).astype(BF16)
        gram_out[...] = before[1][...]
    line = lax.axis_index("yl") * 4 + z
    dx, dh = lax.rem(line // 2 - x + 4, 4), lax.rem(line + h, 2)
    for t, ((ax, ah), _, turn) in enumerate(plan):
        mine, turned = (dx == ax) & (dh == ah), is_turned(turn)
        if turn != "yes":

            @pl.when(mine & jnp.logical_not(turned))
            def _():
                gram_out[...] = g[2 * t + k]

        if turn != "no":
            for side in range(2):

                @pl.when(mine & turned & (k == side))
                def _():
                    gram_out[...] = g[2 * t : 2 * t + 2, :, side * H : (side + 1) * H].reshape(T, H).T


def product(plan, slices, before=()):
    final, count = bool(before), len(plan)
    tiles = [part for _, source, _ in plan for part in source]
    shape = tuple((d, tuple(range(len(source))), turn) for d, source, turn in plan)
    return pl.pallas_call(
        functools.partial(product_kernel, shape, final),
        out_shape=(jax.ShapeDtypeStruct((T, T), BF16 if final else F32), jax.ShapeDtypeStruct((H, T), BF16)),
        in_specs=[VMEM] * (len(tiles) + len(slices) + len(before)),
        out_specs=(VMEM, VMEM),
        scratch_shapes=[pltpu.VMEM((2 * count, H, T), BF16), pltpu.SemaphoreType.DMA((10,))]
        + [pltpu.VMEM((T, T), F32)] * final,
        compiler_params=params(24),
        cost_estimate=cost(2 * count * T * T * T, 4 * count * T * T),
    )(*tiles, *slices, *before)


def sum_core(keep, send):
    other = swap("core")(send)
    return [keep[j].astype(F32) + other[j].astype(F32) for j in range(4)]


def sum_z(sums):
    total = sums[0]
    for j in (1, 3, 2):
        total = total + ring("z", j)(sums[j].astype(BF16)).astype(F32)
    return total.astype(BF16)


def sum_yl(total):
    total = total.astype(F32) + swap("yl")(total).astype(F32)
    return (total * (1.0 / N)).astype(BF16)


def spread(shard):
    n = shard.shape[0] // 2
    one, three = ring("z", -1)(shard), ring("z", 1)(shard)
    mine = [shard, one, three, ring("z", -1)(one[:n]), ring("z", 1)(three[n:])]
    return mine + [swap("core")(a) for a in mine]


def body(quant_codes, block_scales):
    own = dequant(quant_codes, block_scales)

    near1 = ring("x", -1)(own)
    near3 = ring("x", 1)(own)
    far = swap("yh")(own)
    total0 = sum_z(sum_core(*gram(gram_kernel0, 2, [own])))
    top, bottom = halves(near1, near3, total0)
    near2 = (ring("x", -1)(top), ring("x", 1)(bottom))

    total1 = sum_z(sum_core(*gram(gram_kernel1, 5, [own, near1, far], [top])))
    far = gate(far, *near2)
    far1 = ring("x", -1)(far)
    far3 = ring("x", 1)(far)
    sums2 = sum_core(*gram(gram_kernel2, 2, [own, far, *near2], [total1]))

    shard = sum_yl(total1)
    from_x = ring("x", 1)(shard[: 4 * S])
    from_y = swap("yh")(shard[2 * S :])
    line1 = line_up(line_kernel1, 10, [shard, from_x, from_y], [far1, far3])
    slices1 = spread(line1)
    top, bottom = halves(far1, far3, line1)
    far2 = (ring("x", -1)(top), ring("x", 1)(bottom))

    shard = sum_yl(jnp.concatenate([total0, sum_z(sums2)]))
    from_x = ring("x", 2)(shard[2 * S :])
    from_y = swap("yh")(shard[3 * S :])
    slices2 = spread(line_up(line_kernel2, 6, [shard, from_x, from_y], [*slices1[1:3], *far2]))

    plan1 = (
        ((1, 0), (near1,), "no"),
        ((3, 0), (near3,), "yes"),
        ((3, 1), (far3,), "yes"),
        ((1, 1), (far1,), "no"),
        ((0, 1), (far,), "h"),
    )
    plan2 = (((0, 0), (own,), "no"), ((2, 0), near2, "x"), ((2, 1), far2, "x"))
    return product(plan2, slices2, product(plan1, slices1))


def solution(mesh):
    split = Mesh(mesh.devices.reshape(2, 4, 4, 2, 2), AXES)
    line, side = ("yl", "z", "core"), ("x", "yh")
    return jax.shard_map(
        body,
        mesh=split,
        in_specs=(P(line, side), P(side, line)),
        out_specs=(P(line, side), P(line, side)),
        check_vma=False,
    )
```

```python
import functools
import math

import jax
import jax.numpy as jnp
from jax import lax
from jax.experimental import pallas as pl
from jax.experimental.pallas import tpu as pltpu
from jax.sharding import Mesh, PartitionSpec as P

N = 12288
BLOCK = 64
AXES = ("yl", "z", "x", "yh", "core")
F32, BF16 = jnp.float32, jnp.bfloat16
T = 768
H = T // 2
A = H
S = 48
VMEM = pl.BlockSpec(memory_space=pltpu.VMEM)


def ring(axis, step):
    return lambda a: lax.ppermute(a, axis, [(i, (i + step) % 4) for i in range(4)])


def swap(axis):
    return lambda a: lax.ppermute(a, axis, [(0, 1), (1, 0)])


def across(axis, step, other):
    first, axes = AXES.index(axis) < AXES.index(other), sorted((axis, other), key=AXES.index)
    count = 4 if axis in "xz" else 2
    at = (lambda i, o: i * 2 + o) if first else (lambda i, o: o * count + i)
    moves = [(at(i, o), at((i + step) % count, 1 - o)) for i in range(count) for o in range(2)]
    return lambda a: lax.ppermute(a, tuple(axes), moves)


def tdot(a, b):
    return lax.dot_general(a, b, (((0,), (0,)), ((), ())), preferred_element_type=F32)


def dot(a, b):
    return jnp.dot(a, b, preferred_element_type=F32)


def dot_t(a, b):
    return lax.dot_general(a, b, (((1,), (1,)), ((), ())), preferred_element_type=F32)


def params(mib):
    return pltpu.CompilerParams(vmem_limit_bytes=mib << 20)


def cost(flops, size):
    return pl.CostEstimate(flops=flops, bytes_accessed=size, transcendentals=0)


def dequant_kernel(codes, scales, out):
    factor = scales[...].T
    lane = lax.broadcasted_iota(jnp.int32, (T, 128), 1)
    for g in range(T // 128):
        both = jnp.where(lane < BLOCK, factor[:, 2 * g : 2 * g + 1], factor[:, 2 * g + 1 : 2 * g + 2])
        levels = codes[:, 128 * g : 128 * (g + 1)].astype(F32) - 7.5
        out[:, 128 * g : 128 * (g + 1)] = (levels * both).astype(BF16)


def dequant(codes, scales):
    return pl.pallas_call(
        dequant_kernel,
        out_shape=jax.ShapeDtypeStruct((T, T), BF16),
        in_specs=[VMEM, VMEM],
        out_specs=VMEM,
        compiler_params=params(12),
        cost_estimate=cost(2 * T * T, 6 * T * T),
    )(codes, scales)


def cut(full, first, count, keep, send):
    z, k = lax.axis_index("z"), lax.axis_index("core")
    for half in range(count):
        for j in range(4):
            at = half * H + lax.rem(z + j, 4) * S
            to = pl.ds((first + half) * S, S)
            keep[j, to, :] = full[pl.ds(pl.multiple_of(at + k * (4 * S), 16), S), :].astype(BF16)
            send[j, to, :] = full[pl.ds(pl.multiple_of(at + (1 - k) * (4 * S), 16), S), :].astype(BF16)


def gram_kernel0(own, keep, send, full):
    full[...] = tdot(own[...], own[...])
    cut(full, 0, 2, keep, send)


def gram_kernel1(own, near1, far, _, __, ___, keep, send, full):
    turned = near1[...].T
    full[...] = dot(turned, own[...])
    cut(full, 0, 2, keep, send)
    full[...] = dot(turned, far[...])
    cut(full, 2, 2, keep, send)
    h = lax.axis_index("yh")

    @pl.when(h == 0)
    def _():
        full[0:H, :] = tdot(far[:, 0:H], own[...])

    @pl.when(h != 0)
    def _():
        full[0:H, :] = tdot(own[:, H:T], far[...])

    cut(full, 4, 1, keep, send)


def gram_kernel2(own, far, near2a, near2b, _, keep, send, full):
    low = lax.axis_index("x") < 2
    for i, other in enumerate((own, far)):

        @pl.when(low)
        def _():
            full[0:H, :] = tdot(near2a[:, 0:H], other[0:A, :]) + tdot(near2b[:, 0:H], other[A:T, :])

        @pl.when(jnp.logical_not(low))
        def _():
            full[0:H, :] = tdot(other[0:A, H:T], near2a[...]) + tdot(other[A:T, H:T], near2b[...])

        cut(full, i, 1, keep, send)


def gram(kernel, halves, tiles, later=()):
    out = jax.ShapeDtypeStruct((4, halves * S, T), BF16)
    return pl.pallas_call(
        kernel,
        out_shape=(out, out),
        in_specs=[VMEM] * (len(tiles) + len(later)),
        out_specs=(VMEM, VMEM),
        scratch_shapes=[pltpu.VMEM((T, T), F32)],
        compiler_params=params(14),
        cost_estimate=cost(halves * T * T * T, 6 * T * T),
    )(*tiles, *later)


def local(kernel, shapes, *operands):
    out = tuple(jax.ShapeDtypeStruct(shape, BF16) for shape in shapes)
    return pl.pallas_call(
        kernel,
        out_shape=out,
        in_specs=[VMEM] * len(operands),
        out_specs=(VMEM,) * len(out),
        compiler_params=params(12),
        cost_estimate=cost(0, sum(4 * math.prod(shape) for shape in shapes)),
    )(*operands)


def rows_of(value, first, count, *later):
    def kernel(src, *refs):
        refs[-1][...] = src[first : first + count]

    return local(kernel, [(count,) + value.shape[1:]], value, *later)[0]


def gate(value, *later):
    return pl.pallas_call(
        lambda *refs: None,
        out_shape=jax.ShapeDtypeStruct(value.shape, value.dtype),
        in_specs=[VMEM] * (1 + len(later)),
        out_specs=VMEM,
        input_output_aliases={0: 0},
        compiler_params=params(8),
        cost_estimate=cost(0, 0),
    )(value, *later)


def add(*values):
    total = values[0].astype(F32)
    for value in values[1:]:
        total += value.astype(F32)
    return total


def sum_z(keep, send):
    other = swap("core")(send)
    count = keep.shape[1]
    n = count // 32 * 16

    def step1(keep, other, by_up, by_down):
        by_up[...] = add(keep[2, 0:n], other[2, 0:n]).astype(BF16)
        by_down[...] = add(keep[2, n:count], other[2, n:count]).astype(BF16)

    def step2(keep, other, from_down, from_up, up, down):
        up[0:n] = add(keep[1, 0:n], other[1, 0:n], from_down[...]).astype(BF16)
        up[n:count] = add(keep[1, n:count], other[1, n:count]).astype(BF16)
        down[0:n] = add(keep[3, 0:n], other[3, 0:n]).astype(BF16)
        down[n:count] = add(keep[3, n:count], other[3, n:count], from_up[...]).astype(BF16)

    def step3(keep, other, from_down, from_up, out):
        out[...] = add(keep[0], other[0], from_down[...], from_up[...]).astype(BF16)

    up, down = local(step1, [(n, T), (count - n, T)], keep, other)
    up, down = ring("z", 1)(up), ring("z", -1)(down)
    up, down = local(step2, [(count, T)] * 2, keep, other, up, down)
    sent = up
    up, down = ring("z", 1)(up), ring("z", -1)(down)
    return local(step3, [(count, T)], keep, other, up, down)[0], sent


def line_kernel(shard0, shard1, from_x1, from_y1, shard2, from_x2, from_y2, out):
    out[0 : 2 * S] = shard0[...]
    out[2 * S : 4 * S] = shard1[0 : 2 * S]
    out[4 * S : 8 * S] = from_x1[...]
    out[8 * S : 10 * S] = from_y1[0 : 2 * S]
    high = (lax.axis_index("x") >= 2).astype(jnp.int32)
    for at, swapped, mine, theirs in (
        (10, lax.axis_index("yh"), shard1[4 * S : 5 * S], from_y1[2 * S : 3 * S]),
        (12, high, shard2[0:S], from_x2[0:S]),
        (14, high, from_y2[...], from_x2[S : 2 * S]),
    ):
        out[pl.ds(pl.multiple_of((at + swapped) * S, S), S)] = mine
        out[pl.ds(pl.multiple_of((at + 1 - swapped) * S, S), S)] = theirs


RANGES = ((0, 0, 16), (1, 0, 16), (3, 0, 16), (2, 0, 8), (2, 8, 8))


def product_kernel(plan, *refs):
    x, h, z, k = (lax.axis_index(axis) for axis in ("x", "yh", "z", "core"))
    refs = list(refs)
    tiles = [[refs.pop(0) for _ in range(parts)] for _, parts, _ in plan]
    slices = [refs.pop(0) for _ in range(2 * len(RANGES))]
    out, gram_out, g, g_sem, acc = refs

    g_copies = []
    for c in range(2):
        for j, start, size in RANGES:
            core = k if c == 0 else 1 - k
            at = pl.multiple_of(core * (4 * S) + lax.rem(z + j, 4) * S, 16)
            n = len(g_copies)
            g_copies.append(pltpu.make_async_copy(slices[n], g.at[pl.ds(start, size), pl.ds(at, S)], g_sem.at[n]))
    for copy in g_copies:
        copy.start()
    for copy in g_copies:
        copy.wait()

    def tile(t):
        return g[2 * t : 2 * t + 2].reshape(T, T)

    def is_turned(turn):
        return {"no": z < 0, "yes": z >= 0, "h": h != 0, "x": x >= 2}[turn]

    for t, (_, _, turn) in enumerate(plan):
        turned = is_turned(turn)

        def add(multiply):
            at = 0
            for part in tiles[t]:
                rows = slice(at, at + part.shape[0])
                value = multiply(part[...], tile(t))
                if t > 0:
                    acc[rows, :] += value
                else:
                    acc[rows, :] = value
                at += part.shape[0]

        if turn != "yes":

            @pl.when(jnp.logical_not(turned))
            def _():
                add(dot)

        if turn != "no":

            @pl.when(turned)
            def _():
                add(dot_t)

    out[...] = (1.5 * tiles[0][0][...].astype(F32) - 0.5 * acc[...]).astype(BF16)
    line = lax.axis_index("yl") * 4 + z
    dx, dh = lax.rem(line // 2 - x + 4, 4), lax.rem(line + h, 2)
    for t, ((ax, ah), _, turn) in enumerate(plan):
        mine, turned = (dx == ax) & (dh == ah), is_turned(turn)
        if turn != "yes":

            @pl.when(mine & jnp.logical_not(turned))
            def _():
                gram_out[...] = g[2 * t + k]

        if turn != "no":
            for side in range(2):

                @pl.when(mine & turned & (k == side))
                def _():
                    gram_out[...] = g[2 * t : 2 * t + 2, :, side * H : (side + 1) * H].reshape(T, H).T


def product(plan, slices):
    tiles = [part for _, source, _ in plan for part in source]
    shape = tuple((d, len(source), turn) for d, source, turn in plan)
    return pl.pallas_call(
        functools.partial(product_kernel, shape),
        out_shape=(jax.ShapeDtypeStruct((T, T), BF16), jax.ShapeDtypeStruct((H, T), BF16)),
        in_specs=[VMEM] * (len(tiles) + len(slices)),
        out_specs=(VMEM, VMEM),
        scratch_shapes=[
            pltpu.VMEM((16, H, T), BF16),
            pltpu.SemaphoreType.DMA((len(slices),)),
            pltpu.VMEM((T, T), F32),
        ],
        compiler_params=params(26),
        cost_estimate=cost(16 * T * T * T, 36 * T * T),
    )(*tiles, *slices)


def sum_yl(total):
    total = total.astype(F32) + swap("yl")(total).astype(F32)
    return (total * (1.0 / N)).astype(BF16)


def spread(shard, later):
    n = shard.shape[0] // 2
    one, three = ring("z", -1)(shard), ring("z", 1)(shard)
    mine = [shard, one, three]
    mine += [ring("z", -1)(rows_of(one, 0, n, *later)), ring("z", 1)(rows_of(three, n, n, *later))]
    return mine + [swap("core")(a) for a in mine]


def body(quant_codes, block_scales):
    own = dequant(quant_codes, block_scales)

    near1 = ring("x", -1)(own)
    near3 = ring("x", 1)(own)
    far = swap("yh")(own)
    total0, _ = sum_z(*gram(gram_kernel0, 2, [own]))
    down, up = rows_of(near1, 0, H, total0), rows_of(near3, H, H, total0)
    near2 = (ring("x", -1)(down), ring("x", 1)(up))

    total1, sent = sum_z(*gram(gram_kernel1, 5, [own, near1, far], [total0, down, up]))
    total2, _ = sum_z(*gram(gram_kernel2, 2, [own, far, *near2], [sent]))
    shard0, shard1, shard2 = sum_yl(total0), sum_yl(total1), sum_yl(total2)
    from_x1 = ring("x", 1)(shard1[: 4 * S])
    from_y1 = swap("yh")(shard1[2 * S :])
    from_x2 = ring("x", 2)(shard2)
    from_y2 = swap("yh")(shard2[S:])
    line = local(line_kernel, [(16 * S, T)], shard0, shard1, from_x1, from_y1, shard2, from_x2, from_y2)[0]

    def stack(top, bottom, _, out):
        out[0:H] = top[...]
        out[H:T] = bottom[...]

    again = rows_of(far, 0, T, line)
    far1, far3 = ring("x", -1)(again), ring("x", 1)(again)
    far2 = swap("yh")(local(stack, [(T, T)], *near2, line)[0])
    slices = spread(line.reshape(16, S, T), (far1, far2, far3))

    plan = (
        ((0, 0), (own,), "no"),
        ((1, 0), (near1,), "no"),
        ((3, 0), (near3,), "yes"),
        ((3, 1), (far3,), "yes"),
        ((1, 1), (far1,), "no"),
        ((0, 1), (far,), "h"),
        ((2, 0), near2, "x"),
        ((2, 1), (far2,), "x"),
    )
    return product(plan, slices)


def solution(mesh):
    split = Mesh(mesh.devices.reshape(2, 4, 4, 2, 2), AXES)
    line, side = ("yl", "z", "core"), ("x", "yh")
    return jax.shard_map(
        body,
        mesh=split,
        in_specs=(P(line, side), P(side, line)),
        out_specs=(P(line, side), P(line, side)),
        check_vma=False,
    )
```

```python
import math

import jax
import jax.numpy as jnp
from jax import lax
from jax.experimental import pallas as pl
from jax.experimental.pallas import tpu as pltpu
from jax.sharding import Mesh, PartitionSpec as P

N = 12288
BLOCK = 64
AXES = ("yl", "z", "x", "yh", "core")
F32, BF16 = jnp.float32, jnp.bfloat16
T = 768
H = T // 2
A = H
S = 48
VMEM = pl.BlockSpec(memory_space=pltpu.VMEM)


def ring(axis, step):
    return lambda a: lax.ppermute(a, axis, [(i, (i + step) % 4) for i in range(4)])


def swap(axis):
    return lambda a: lax.ppermute(a, axis, [(0, 1), (1, 0)])


def across(axis, step, other):
    first, axes = AXES.index(axis) < AXES.index(other), sorted((axis, other), key=AXES.index)
    count = 4 if axis in "xz" else 2
    at = (lambda i, o: i * 2 + o) if first else (lambda i, o: o * count + i)
    moves = [(at(i, o), at((i + step) % count, 1 - o)) for i in range(count) for o in range(2)]
    return lambda a: lax.ppermute(a, tuple(axes), moves)


def tdot(a, b):
    return lax.dot_general(a, b, (((0,), (0,)), ((), ())), preferred_element_type=F32)


def dot(a, b):
    return jnp.dot(a, b, preferred_element_type=F32)


def dot_t(a, b):
    return lax.dot_general(a, b, (((1,), (1,)), ((), ())), preferred_element_type=F32)


def params(mib):
    return pltpu.CompilerParams(vmem_limit_bytes=mib << 20)


def cost(flops, size):
    return pl.CostEstimate(flops=flops, bytes_accessed=size, transcendentals=0)


def dequant_kernel(codes, scales, out):
    factor = scales[...].T
    lane = lax.broadcasted_iota(jnp.int32, (T, 128), 1)
    for g in range(T // 128):
        both = jnp.where(lane < BLOCK, factor[:, 2 * g : 2 * g + 1], factor[:, 2 * g + 1 : 2 * g + 2])
        levels = codes[:, 128 * g : 128 * (g + 1)].astype(F32) - 7.5
        out[:, 128 * g : 128 * (g + 1)] = (levels * both).astype(BF16)


def dequant(codes, scales):
    return pl.pallas_call(
        dequant_kernel,
        out_shape=jax.ShapeDtypeStruct((T, T), BF16),
        in_specs=[VMEM, VMEM],
        out_specs=VMEM,
        compiler_params=params(12),
        cost_estimate=cost(2 * T * T, 6 * T * T),
    )(codes, scales)


def cut(full, first, count, keep, send):
    z, k = lax.axis_index("z"), lax.axis_index("core")
    for half in range(count):
        for j in range(4):
            at = half * H + lax.rem(z + j, 4) * S
            to = pl.ds((first + half) * S, S)
            keep[j, to, :] = full[pl.ds(pl.multiple_of(at + k * (4 * S), 16), S), :].astype(BF16)
            send[j, to, :] = full[pl.ds(pl.multiple_of(at + (1 - k) * (4 * S), 16), S), :].astype(BF16)


def gram_kernel0(own, keep, send, full):
    full[...] = tdot(own[...], own[...])
    cut(full, 0, 2, keep, send)


def gram_kernel1(own, near1, far, _, __, ___, keep, send, full):
    turned = near1[...].T
    full[...] = dot(turned, own[...])
    cut(full, 0, 2, keep, send)
    full[...] = dot(turned, far[...])
    cut(full, 2, 2, keep, send)
    h = lax.axis_index("yh")

    @pl.when(h == 0)
    def _():
        full[0:H, :] = tdot(far[:, 0:H], own[...])

    @pl.when(h != 0)
    def _():
        full[0:H, :] = tdot(own[:, H:T], far[...])

    cut(full, 4, 1, keep, send)


def gram_kernel2(own, far, near2a, near2b, _, keep, send, full):
    low = lax.axis_index("x") < 2
    for i, other in enumerate((own, far)):

        @pl.when(low)
        def _():
            full[0:H, :] = tdot(near2a[:, 0:H], other[0:A, :]) + tdot(near2b[:, 0:H], other[A:T, :])

        @pl.when(jnp.logical_not(low))
        def _():
            full[0:H, :] = tdot(other[0:A, H:T], near2a[...]) + tdot(other[A:T, H:T], near2b[...])

        cut(full, i, 1, keep, send)


def gram(kernel, halves, tiles, later=()):
    out = jax.ShapeDtypeStruct((4, halves * S, T), BF16)
    return pl.pallas_call(
        kernel,
        out_shape=(out, out),
        in_specs=[VMEM] * (len(tiles) + len(later)),
        out_specs=(VMEM, VMEM),
        scratch_shapes=[pltpu.VMEM((T, T), F32)],
        compiler_params=params(14),
        cost_estimate=cost(halves * T * T * T, 6 * T * T),
    )(*tiles, *later)


def local(kernel, shapes, *operands):
    out = tuple(jax.ShapeDtypeStruct(shape, BF16) for shape in shapes)
    return pl.pallas_call(
        kernel,
        out_shape=out,
        in_specs=[VMEM] * len(operands),
        out_specs=(VMEM,) * len(out),
        compiler_params=params(12),
        cost_estimate=cost(0, sum(4 * math.prod(shape) for shape in shapes)),
    )(*operands)


def rows_of(value, first, count, *later):
    def kernel(src, *refs):
        refs[-1][...] = src[first : first + count]

    return local(kernel, [(count,) + value.shape[1:]], value, *later)[0]


def gate(value, *later):
    return pl.pallas_call(
        lambda *refs: None,
        out_shape=jax.ShapeDtypeStruct(value.shape, value.dtype),
        in_specs=[VMEM] * (1 + len(later)),
        out_specs=VMEM,
        input_output_aliases={0: 0},
        compiler_params=params(8),
        cost_estimate=cost(0, 0),
    )(value, *later)


def add(*values):
    total = values[0].astype(F32)
    for value in values[1:]:
        total += value.astype(F32)
    return total


def sum_z_in_steps(keep, send):
    other = swap("core")(send)
    count = keep.shape[1]
    n = count // 32 * 16

    def step1(keep, other, by_up, by_down):
        by_up[...] = add(keep[2, 0:n], other[2, 0:n]).astype(BF16)
        by_down[...] = add(keep[2, n:count], other[2, n:count]).astype(BF16)

    def step2(keep, other, from_down, from_up, up, down):
        up[0:n] = add(keep[1, 0:n], other[1, 0:n], from_down[...]).astype(BF16)
        up[n:count] = add(keep[1, n:count], other[1, n:count]).astype(BF16)
        down[0:n] = add(keep[3, 0:n], other[3, 0:n]).astype(BF16)
        down[n:count] = add(keep[3, n:count], other[3, n:count], from_up[...]).astype(BF16)

    def step3(keep, other, from_down, from_up, out):
        out[...] = add(keep[0], other[0], from_down[...], from_up[...]).astype(BF16)

    up, down = local(step1, [(n, T), (count - n, T)], keep, other)
    up, down = ring("z", 1)(up), ring("z", -1)(down)
    up, down = local(step2, [(count, T)] * 2, keep, other, up, down)
    up, down = ring("z", 1)(up), ring("z", -1)(down)
    return local(step3, [(count, T)], keep, other, up, down)[0]


def sum_z(keep, send):
    other = swap("core")(send)
    shape = keep.shape[1:]

    def step1(keep, other, *parts):
        for j, part in enumerate(parts):
            part[...] = add(keep[j + 1], other[j + 1]).astype(BF16)

    def step2(keep, other, one, three, two, out):
        out[...] = add(keep[0], other[0], one[...], three[...], two[...]).astype(BF16)

    parts = local(step1, [shape] * 3, keep, other)
    got = [ring("z", j)(parts[j - 1]) for j in (1, 3, 2)]
    return local(step2, [shape], keep, other, *got)[0]


def line_kernel(shard0, shard1, from_x1, shard2, from_x2, from_y, out):
    out[0 : 2 * S] = shard0[...]
    out[2 * S : 4 * S] = shard1[0 : 2 * S]
    out[4 * S : 6 * S] = from_y[0 : 2 * S]
    out[6 * S : 10 * S] = from_x1[...]
    high = (lax.axis_index("x") >= 2).astype(jnp.int32)
    for at, swapped, mine, theirs in (
        (10, lax.axis_index("yh"), shard1[4 * S : 5 * S], from_y[2 * S : 3 * S]),
        (12, high, shard2[0:S], from_x2[0:S]),
        (14, high, from_y[3 * S : 4 * S], from_x2[S : 2 * S]),
    ):
        out[pl.ds(pl.multiple_of((at + swapped) * S, S), S)] = mine
        out[pl.ds(pl.multiple_of((at + 1 - swapped) * S, S), S)] = theirs


RANGES = ((0, 0, 16), (1, 0, 16), (3, 0, 16), (2, 0, 8), (2, 8, 8))


TILES = (
    ((0, 0), "no"),
    ((1, 0), "no"),
    ((1, 1), "no"),
    ((3, 0), "yes"),
    ((3, 1), "yes"),
    ((0, 1), "h"),
    ((2, 0), "x"),
    ((2, 1), "x"),
)


def product_kernel(own, near1, far1, near3, far3, far, near2a, near2b, far2, *refs):
    x, h, z, k = (lax.axis_index(axis) for axis in ("x", "yh", "z", "core"))
    slices, (out, gram_out, g, g_sem, acc) = refs[:10], refs[10:]

    g_copies = []
    for c in range(2):
        for j, start, size in RANGES:
            core = k if c == 0 else 1 - k
            at = pl.multiple_of(core * (4 * S) + lax.rem(z + j, 4) * S, 16)
            n = len(g_copies)
            g_copies.append(pltpu.make_async_copy(slices[n], g.at[pl.ds(start, size), pl.ds(at, S)], g_sem.at[n]))
    for copy in g_copies:
        copy.start()
    for copy in g_copies:
        copy.wait()

    def tiles(first, count):
        return g[2 * first : 2 * (first + count)].reshape(count * T, T)

    def beside(parts):
        return jnp.concatenate(parts, axis=1)

    def either(turned, straight_way, turned_way):
        pl.when(jnp.logical_not(turned))(straight_way)
        pl.when(turned)(turned_way)

    def far_straight():
        acc[...] = dot(far[...], tiles(5, 1))

    def far_turned():
        acc[...] = dot_t(far[...], tiles(5, 1))

    either(h != 0, far_straight, far_turned)
    acc[...] += dot(beside([own[...], near1[...], far1[...]]), tiles(0, 3))
    acc[...] += dot_t(beside([near3[...], far3[...]]), beside([tiles(3, 1), tiles(4, 1)]))

    def finish(multiply, factor):
        for i, near2 in enumerate((near2a, near2b)):
            rows = slice(i * H, (i + 1) * H)
            total = acc[rows, :] + multiply(beside([near2[...], far2[rows, :]]), factor)
            out[rows, :] = (1.5 * own[rows, :].astype(F32) - 0.5 * total).astype(BF16)

    either(
        x >= 2,
        lambda: finish(dot, tiles(6, 2)),
        lambda: finish(dot_t, beside([tiles(6, 1), tiles(7, 1)])),
    )

    line = lax.axis_index("yl") * 4 + z
    dx, dh = lax.rem(line // 2 - x + 4, 4), lax.rem(line + h, 2)
    for t, ((ax, ah), turn) in enumerate(TILES):
        mine, turned = (dx == ax) & (dh == ah), {"no": z < 0, "yes": z >= 0, "h": h != 0, "x": x >= 2}[turn]
        if turn != "yes":

            @pl.when(mine & jnp.logical_not(turned))
            def _():
                gram_out[...] = g[2 * t + k]

        if turn != "no":
            for side in range(2):

                @pl.when(mine & turned & (k == side))
                def _():
                    gram_out[...] = g[2 * t : 2 * t + 2, :, side * H : (side + 1) * H].reshape(T, H).T


def product(tiles, slices):
    operands = [*tiles, *slices]
    return pl.pallas_call(
        product_kernel,
        out_shape=(jax.ShapeDtypeStruct((T, T), BF16), jax.ShapeDtypeStruct((H, T), BF16)),
        in_specs=[VMEM] * len(operands),
        out_specs=(VMEM, VMEM),
        scratch_shapes=[
            pltpu.VMEM((16, H, T), BF16),
            pltpu.SemaphoreType.DMA((len(slices),)),
            pltpu.VMEM((T, T), F32),
        ],
        compiler_params=params(30),
        cost_estimate=cost(16 * T * T * T, 36 * T * T),
    )(*operands)


def sum_yl(total):
    total = total.astype(F32) + swap("yl")(total).astype(F32)
    return (total * (1.0 / N)).astype(BF16)


def spread(shard, later):
    n = shard.shape[0] // 2
    one, three = ring("z", -1)(shard), ring("z", 1)(shard)
    mine = [shard, one, three]
    mine += [ring("z", -1)(rows_of(one, 0, n, *later)), ring("z", 1)(rows_of(three, n, n, *later))]
    return mine + [swap("core")(a) for a in mine]


def body(quant_codes, block_scales):
    own = dequant(quant_codes, block_scales)

    near1 = ring("x", -1)(own)
    near3 = ring("x", 1)(own)
    far = swap("yh")(own)
    total0 = sum_z_in_steps(*gram(gram_kernel0, 2, [own]))
    down, up = rows_of(near1, 0, H, total0), rows_of(near3, H, H, total0)
    near2 = (ring("x", -1)(down), ring("x", 1)(up))

    total1 = sum_z(*gram(gram_kernel1, 5, [own, near1, far], [total0, down, up]))
    total2 = sum_z(*gram(gram_kernel2, 2, [own, far, *near2], [total1]))
    shard0, shard1, shard2 = sum_yl(total0), sum_yl(total1), sum_yl(total2)
    from_x1 = ring("x", 1)(shard1[: 4 * S])
    from_x2 = ring("x", 2)(shard2)

    def to_y(first, second, out):
        out[0 : 3 * S] = first[2 * S : 5 * S]
        out[3 * S : 4 * S] = second[S : 2 * S]

    from_y = swap("yh")(local(to_y, [(4 * S, T)], shard1, shard2)[0])
    line = local(line_kernel, [(16 * S, T)], shard0, shard1, from_x1, shard2, from_x2, from_y)[0]

    def stack(top, bottom, _, out):
        out[0:H] = top[...]
        out[H:T] = bottom[...]

    again = rows_of(far, 0, T, line)
    far1, far3 = ring("x", -1)(again), ring("x", 1)(again)
    far2 = swap("yh")(local(stack, [(T, T)], *near2, line)[0])
    slices = spread(line.reshape(16, S, T), (far1, far2, far3))

    return product([own, near1, far1, near3, far3, far, *near2, far2], slices)


def solution(mesh):
    split = Mesh(mesh.devices.reshape(2, 4, 4, 2, 2), AXES)
    line, side = ("yl", "z", "core"), ("x", "yh")
    return jax.shard_map(
        body,
        mesh=split,
        in_specs=(P(line, side), P(side, line)),
        out_specs=(P(line, side), P(line, side)),
        check_vma=False,
    )
```

```python
import math

import jax
import jax.numpy as jnp
from jax import lax
from jax.experimental import pallas as pl
from jax.experimental.pallas import tpu as pltpu
from jax.sharding import Mesh, PartitionSpec as P

N = 12288
BLOCK = 64
AXES = ("yl", "z", "x", "yh", "core")
F32, BF16 = jnp.float32, jnp.bfloat16
T = 768
H = T // 2
A = H
S = 48
VMEM = pl.BlockSpec(memory_space=pltpu.VMEM)
ANY = pl.BlockSpec(memory_space=pl.ANY)


def ring(axis, step):
    return lambda a: lax.ppermute(a, axis, [(i, (i + step) % 4) for i in range(4)])


def swap(axis):
    return lambda a: lax.ppermute(a, axis, [(0, 1), (1, 0)])


def across(axis, step, other):
    first, axes = AXES.index(axis) < AXES.index(other), sorted((axis, other), key=AXES.index)
    count = 4 if axis in "xz" else 2
    at = (lambda i, o: i * 2 + o) if first else (lambda i, o: o * count + i)
    moves = [(at(i, o), at((i + step) % count, 1 - o)) for i in range(count) for o in range(2)]
    return lambda a: lax.ppermute(a, tuple(axes), moves)


def tdot(a, b):
    return lax.dot_general(a, b, (((0,), (0,)), ((), ())), preferred_element_type=F32)


def dot(a, b):
    return jnp.dot(a, b, preferred_element_type=F32)


def dot_t(a, b):
    return lax.dot_general(a, b, (((1,), (1,)), ((), ())), preferred_element_type=F32)


def params(mib):
    return pltpu.CompilerParams(vmem_limit_bytes=mib << 20)


def cost(flops, size):
    return pl.CostEstimate(flops=flops, bytes_accessed=size, transcendentals=0)


def dequant_kernel(codes, scales, out):
    factor = scales[...].T
    lane = lax.broadcasted_iota(jnp.int32, (T, 128), 1)
    for g in range(T // 128):
        both = jnp.where(lane < BLOCK, factor[:, 2 * g : 2 * g + 1], factor[:, 2 * g + 1 : 2 * g + 2])
        levels = codes[:, 128 * g : 128 * (g + 1)].astype(F32) - 7.5
        out[:, 128 * g : 128 * (g + 1)] = (levels * both).astype(BF16)


def dequant(codes, scales):
    return pl.pallas_call(
        dequant_kernel,
        out_shape=jax.ShapeDtypeStruct((T, T), BF16),
        in_specs=[VMEM, VMEM],
        out_specs=VMEM,
        compiler_params=params(12),
        cost_estimate=cost(2 * T * T, 6 * T * T),
    )(codes, scales)


def cut(full, first, count, keep, send):
    z, k = lax.axis_index("z"), lax.axis_index("core")
    for half in range(count):
        for j in range(4):
            at = half * H + lax.rem(z + j, 4) * S
            to = pl.ds((first + half) * S, S)
            keep[j, to, :] = full[pl.ds(pl.multiple_of(at + k * (4 * S), 16), S), :].astype(BF16)
            send[j, to, :] = full[pl.ds(pl.multiple_of(at + (1 - k) * (4 * S), 16), S), :].astype(BF16)


def gram_kernel0(own, keep, send, full):
    full[...] = tdot(own[...], own[...])
    cut(full, 0, 2, keep, send)


def gram_kernel1(own, near1, far, _, __, ___, keep, send, full):
    turned = near1[...].T
    full[...] = dot(turned, own[...])
    cut(full, 0, 2, keep, send)
    full[...] = dot(turned, far[...])
    cut(full, 2, 2, keep, send)
    h = lax.axis_index("yh")

    @pl.when(h == 0)
    def _():
        full[0:H, :] = tdot(far[:, 0:H], own[...])

    @pl.when(h != 0)
    def _():
        full[0:H, :] = tdot(own[:, H:T], far[...])

    cut(full, 4, 1, keep, send)


def gram_kernel2(own, far, near2a, near2b, _, keep, send, full):
    low = lax.axis_index("x") < 2
    for i, other in enumerate((own, far)):

        @pl.when(low)
        def _():
            full[0:H, :] = tdot(near2a[:, 0:H], other[0:A, :]) + tdot(near2b[:, 0:H], other[A:T, :])

        @pl.when(jnp.logical_not(low))
        def _():
            full[0:H, :] = tdot(other[0:A, H:T], near2a[...]) + tdot(other[A:T, H:T], near2b[...])

        cut(full, i, 1, keep, send)


def gram(kernel, halves, tiles, later=()):
    out = jax.ShapeDtypeStruct((4, halves * S, T), BF16)
    return pl.pallas_call(
        kernel,
        out_shape=(out, out),
        in_specs=[VMEM] * (len(tiles) + len(later)),
        out_specs=(VMEM, VMEM),
        scratch_shapes=[pltpu.VMEM((T, T), F32)],
        compiler_params=params(14),
        cost_estimate=cost(halves * T * T * T, 6 * T * T),
    )(*tiles, *later)


def local(kernel, shapes, *operands):
    out = tuple(jax.ShapeDtypeStruct(shape, BF16) for shape in shapes)
    return pl.pallas_call(
        kernel,
        out_shape=out,
        in_specs=[VMEM] * len(operands),
        out_specs=(VMEM,) * len(out),
        compiler_params=params(12),
        cost_estimate=cost(0, sum(4 * math.prod(shape) for shape in shapes)),
    )(*operands)


def rows_of(value, first, count, *later):
    def kernel(src, *refs):
        refs[-1][...] = src[first : first + count]

    return local(kernel, [(count,) + value.shape[1:]], value, *later)[0]


def gate(value, *later):
    return pl.pallas_call(
        lambda *refs: None,
        out_shape=jax.ShapeDtypeStruct(value.shape, value.dtype),
        in_specs=[VMEM] * (1 + len(later)),
        out_specs=VMEM,
        input_output_aliases={0: 0},
        compiler_params=params(8),
        cost_estimate=cost(0, 0),
    )(value, *later)


def add(*values):
    total = values[0].astype(F32)
    for value in values[1:]:
        total += value.astype(F32)
    return total


def sum_z_in_steps(keep, send):
    other = swap("core")(send)
    count = keep.shape[1]
    n = count // 32 * 16

    def step1(keep, other, by_up, by_down):
        by_up[...] = add(keep[2, 0:n], other[2, 0:n]).astype(BF16)
        by_down[...] = add(keep[2, n:count], other[2, n:count]).astype(BF16)

    def step2(keep, other, from_down, from_up, up, down):
        up[0:n] = add(keep[1, 0:n], other[1, 0:n], from_down[...]).astype(BF16)
        up[n:count] = add(keep[1, n:count], other[1, n:count]).astype(BF16)
        down[0:n] = add(keep[3, 0:n], other[3, 0:n]).astype(BF16)
        down[n:count] = add(keep[3, n:count], other[3, n:count], from_up[...]).astype(BF16)

    def step3(keep, other, from_down, from_up, out):
        out[...] = add(keep[0], other[0], from_down[...], from_up[...]).astype(BF16)

    up, down = local(step1, [(n, T), (count - n, T)], keep, other)
    up, down = ring("z", 1)(up), ring("z", -1)(down)
    up, down = local(step2, [(count, T)] * 2, keep, other, up, down)
    up, down = ring("z", 1)(up), ring("z", -1)(down)
    return local(step3, [(count, T)], keep, other, up, down)[0]


def sum_z(keep, send):
    other = swap("core")(send)
    shape = keep.shape[1:]

    def step1(keep, other, *parts):
        for j, part in enumerate(parts):
            part[...] = add(keep[j + 1], other[j + 1]).astype(BF16)

    def step2(keep, other, one, three, two, out):
        out[...] = add(keep[0], other[0], one[...], three[...], two[...]).astype(BF16)

    parts = local(step1, [shape] * 3, keep, other)
    got = [ring("z", j)(parts[j - 1]) for j in (1, 3, 2)]
    return local(step2, [shape], keep, other, *got)[0]


def line_kernel(shard0, shard1, from_x1, shard2, from_x2, from_y, out):
    out[0 : 2 * S] = shard0[...]
    out[2 * S : 4 * S] = shard1[0 : 2 * S]
    out[4 * S : 6 * S] = from_y[0 : 2 * S]
    out[6 * S : 10 * S] = from_x1[...]
    high = (lax.axis_index("x") >= 2).astype(jnp.int32)
    for at, swapped, mine, theirs in (
        (10, lax.axis_index("yh"), shard1[4 * S : 5 * S], from_y[2 * S : 3 * S]),
        (12, high, shard2[0:S], from_x2[0:S]),
        (14, high, from_y[3 * S : 4 * S], from_x2[S : 2 * S]),
    ):
        out[pl.ds(pl.multiple_of((at + swapped) * S, S), S)] = mine
        out[pl.ds(pl.multiple_of((at + 1 - swapped) * S, S), S)] = theirs


RANGES = ((0, 0, 16), (1, 0, 16), (3, 0, 16), (2, 0, 8), (2, 8, 8))


TILES = (
    ((0, 0), "no"),
    ((1, 0), "no"),
    ((1, 1), "no"),
    ((3, 0), "yes"),
    ((3, 1), "yes"),
    ((0, 1), "h"),
    ((2, 0), "x"),
    ((2, 1), "x"),
)


def product_kernel(own, near1, far1, near3, far3, far, near2a, near2b, far2, *refs):
    x, h, z, k = (lax.axis_index(axis) for axis in ("x", "yh", "z", "core"))
    slices, (out_far, gram_far, g, g_sem, acc, out, gram_out, sems) = refs[:10], refs[10:]

    g_copies = []
    for c in range(2):
        for j, start, size in RANGES:
            core = k if c == 0 else 1 - k
            at = pl.multiple_of(core * (4 * S) + lax.rem(z + j, 4) * S, 16)
            n = len(g_copies)
            g_copies.append(pltpu.make_async_copy(slices[n], g.at[pl.ds(start, size), pl.ds(at, S)], g_sem.at[n]))
    for copy in g_copies:
        copy.start()
    for copy in g_copies:
        copy.wait()

    def tiles(first, count):
        return g[2 * first : 2 * (first + count)].reshape(count * T, T)

    def beside(parts):
        return jnp.concatenate(parts, axis=1)

    def either(turned, straight_way, turned_way):
        pl.when(jnp.logical_not(turned))(straight_way)
        pl.when(turned)(turned_way)

    line = lax.axis_index("yl") * 4 + z
    dx, dh = lax.rem(line // 2 - x + 4, 4), lax.rem(line + h, 2)
    for t, ((ax, ah), turn) in enumerate(TILES):
        mine, turned = (dx == ax) & (dh == ah), {"no": z < 0, "yes": z >= 0, "h": h != 0, "x": x >= 2}[turn]
        if turn != "yes":

            @pl.when(mine & jnp.logical_not(turned))
            def _():
                gram_out[...] = g[2 * t + k]

        if turn != "no":
            for side in range(2):

                @pl.when(mine & turned & (k == side))
                def _():
                    gram_out[...] = g[2 * t : 2 * t + 2, :, side * H : (side + 1) * H].reshape(T, H).T

    copies = [pltpu.make_async_copy(gram_out, gram_far, sems.at[2])]
    for i in range(2):
        rows = pl.ds(i * H, H)
        copies.append(pltpu.make_async_copy(out.at[rows], out_far.at[rows], sems.at[i]))
    copies[0].start()

    def far_straight():
        acc[...] = dot(far[...], tiles(5, 1))

    def far_turned():
        acc[...] = dot_t(far[...], tiles(5, 1))

    either(h != 0, far_straight, far_turned)
    acc[...] += dot(beside([own[...], near1[...], far1[...]]), tiles(0, 3))
    acc[...] += dot_t(beside([near3[...], far3[...]]), beside([tiles(3, 1), tiles(4, 1)]))

    def finish(multiply, factor):
        for i, near2 in enumerate((near2a, near2b)):
            rows = slice(i * H, (i + 1) * H)
            total = acc[rows, :] + multiply(beside([near2[...], far2[rows, :]]), factor)
            out[rows, :] = (1.5 * own[rows, :].astype(F32) - 0.5 * total).astype(BF16)
            copies[1 + i].start()

    either(
        x >= 2,
        lambda: finish(dot, tiles(6, 2)),
        lambda: finish(dot_t, beside([tiles(6, 1), tiles(7, 1)])),
    )
    for copy in copies:
        copy.wait()


def product(tiles, slices):
    operands = [*tiles, *slices]
    return pl.pallas_call(
        product_kernel,
        out_shape=(jax.ShapeDtypeStruct((T, T), BF16), jax.ShapeDtypeStruct((H, T), BF16)),
        in_specs=[VMEM] * len(operands),
        out_specs=(ANY, ANY),
        scratch_shapes=[
            pltpu.VMEM((16, H, T), BF16),
            pltpu.SemaphoreType.DMA((len(slices),)),
            pltpu.VMEM((T, T), F32),
            pltpu.VMEM((T, T), BF16),
            pltpu.VMEM((H, T), BF16),
            pltpu.SemaphoreType.DMA((3,)),
        ],
        compiler_params=params(30),
        cost_estimate=cost(16 * T * T * T, 36 * T * T),
    )(*operands)


def sum_yl(total):
    total = total.astype(F32) + swap("yl")(total).astype(F32)
    return (total * (1.0 / N)).astype(BF16)


def body(quant_codes, block_scales):
    own = dequant(quant_codes, block_scales)

    near1 = ring("x", -1)(own)
    near3 = ring("x", 1)(own)
    far = swap("yh")(own)
    total0 = sum_z_in_steps(*gram(gram_kernel0, 2, [own]))
    down, up = rows_of(near1, 0, H, total0, far), rows_of(near3, H, H, total0, far)
    near2 = (ring("x", -1)(down), ring("x", 1)(up))

    total1 = sum_z(*gram(gram_kernel1, 5, [own, near1, far], [total0, down, up]))
    total2 = sum_z(*gram(gram_kernel2, 2, [own, far, *near2], [total1]))
    shard0, shard1, shard2 = sum_yl(total0), sum_yl(total1), sum_yl(total2)
    from_x1 = ring("x", 1)(shard1[: 4 * S])
    from_x2 = ring("x", 2)(shard2)

    def to_y(first, second, out):
        out[0 : 3 * S] = first[2 * S : 5 * S]
        out[3 * S : 4 * S] = second[S : 2 * S]

    from_y = swap("yh")(local(to_y, [(4 * S, T)], shard1, shard2)[0])
    line = local(line_kernel, [(16 * S, T)], shard0, shard1, from_x1, shard2, from_x2, from_y)[0]

    def stack(top, bottom, _, out):
        out[0:H] = top[...]
        out[H:T] = bottom[...]

    again = rows_of(far, 0, T, line)
    far1, far3 = ring("x", -1)(again), ring("x", 1)(again)
    far2 = swap("yh")(local(stack, [(T, T)], *near2, line)[0])
    line = line.reshape(16, S, T)
    one, three = ring("z", -1)(line), ring("z", 1)(line)
    two = [ring("z", -1)(rows_of(one, 0, 8)), ring("z", 1)(rows_of(three, 8, 8))]
    two = [gate(a, far1, far2, far3) for a in two]
    mine = [line, one, three, *two]
    slices = mine + [swap("core")(a) for a in mine]
    return product([own, near1, far1, near3, far3, far, *near2, far2], slices)


def solution(mesh):
    split = Mesh(mesh.devices.reshape(2, 4, 4, 2, 2), AXES)
    line, side = ("yl", "z", "core"), ("x", "yh")
    return jax.shard_map(
        body,
        mesh=split,
        in_specs=(P(line, side), P(side, line)),
        out_specs=(P(line, side), P(line, side)),
        check_vma=False,
    )
```

```python
import math

import jax
import jax.numpy as jnp
from jax import lax
from jax.experimental import pallas as pl
from jax.experimental.pallas import tpu as pltpu
from jax.sharding import Mesh, PartitionSpec as P

N = 12288
BLOCK = 64
AXES = ("yl", "z", "x", "yh", "core")
F32, BF16 = jnp.float32, jnp.bfloat16
T = 768
H = T // 2
A = H
S = 48
VMEM = pl.BlockSpec(memory_space=pltpu.VMEM)
ANY = pl.BlockSpec(memory_space=pl.ANY)


def ring(axis, step):
    return lambda a: lax.ppermute(a, axis, [(i, (i + step) % 4) for i in range(4)])


def swap(axis):
    return lambda a: lax.ppermute(a, axis, [(0, 1), (1, 0)])


def across(axis, step, other):
    first, axes = AXES.index(axis) < AXES.index(other), sorted((axis, other), key=AXES.index)
    count = 4 if axis in "xz" else 2
    at = (lambda i, o: i * 2 + o) if first else (lambda i, o: o * count + i)
    moves = [(at(i, o), at((i + step) % count, 1 - o)) for i in range(count) for o in range(2)]
    return lambda a: lax.ppermute(a, tuple(axes), moves)


def tdot(a, b):
    return lax.dot_general(a, b, (((0,), (0,)), ((), ())), preferred_element_type=F32)


def dot(a, b):
    return jnp.dot(a, b, preferred_element_type=F32)


def dot_t(a, b):
    return lax.dot_general(a, b, (((1,), (1,)), ((), ())), preferred_element_type=F32)


def params(mib):
    return pltpu.CompilerParams(vmem_limit_bytes=mib << 20)


def cost(flops, size):
    return pl.CostEstimate(flops=flops, bytes_accessed=size, transcendentals=0)


def dequant_kernel(codes, scales, out):
    factor = scales[...].T
    lane = lax.broadcasted_iota(jnp.int32, (T, 128), 1)
    for g in range(T // 128):
        both = jnp.where(lane < BLOCK, factor[:, 2 * g : 2 * g + 1], factor[:, 2 * g + 1 : 2 * g + 2])
        levels = codes[:, 128 * g : 128 * (g + 1)].astype(F32) - 7.5
        out[:, 128 * g : 128 * (g + 1)] = (levels * both).astype(BF16)


def dequant(codes, scales):
    return pl.pallas_call(
        dequant_kernel,
        out_shape=jax.ShapeDtypeStruct((T, T), BF16),
        in_specs=[VMEM, VMEM],
        out_specs=VMEM,
        compiler_params=params(12),
        cost_estimate=cost(2 * T * T, 6 * T * T),
    )(codes, scales)


def cut(full, first, count, keep, send):
    z, k = lax.axis_index("z"), lax.axis_index("core")
    for half in range(count):
        for j in range(4):
            at = half * H + lax.rem(z + j, 4) * S
            to = pl.ds((first + half) * S, S)
            keep[j, to, :] = full[pl.ds(pl.multiple_of(at + k * (4 * S), 16), S), :].astype(BF16)
            send[j, to, :] = full[pl.ds(pl.multiple_of(at + (1 - k) * (4 * S), 16), S), :].astype(BF16)


def gram_kernel0(own, keep, send, full):
    full[...] = tdot(own[...], own[...])
    cut(full, 0, 2, keep, send)


def gram_kernel1a(own, near1, far, _, __, ___, keep, send, full):
    full[...] = tdot(near1[...], own[...])
    cut(full, 0, 2, keep, send)
    h = lax.axis_index("yh")

    @pl.when(h == 0)
    def _():
        full[0:H, :] = tdot(far[:, 0:H], own[...])

    @pl.when(h != 0)
    def _():
        full[0:H, :] = tdot(own[:, H:T], far[...])

    cut(full, 2, 1, keep, send)


def gram_kernel1b(near1, far, _, keep, send, full):
    full[...] = tdot(near1[...], far[...])
    cut(full, 0, 2, keep, send)


def gram_kernel2(own, far, near2a, near2b, _, keep, send, full):
    low = lax.axis_index("x") < 2
    for i, other in enumerate((own, far)):

        @pl.when(low)
        def _():
            full[0:H, :] = tdot(near2a[:, 0:H], other[0:A, :]) + tdot(near2b[:, 0:H], other[A:T, :])

        @pl.when(jnp.logical_not(low))
        def _():
            full[0:H, :] = tdot(other[0:A, H:T], near2a[...]) + tdot(other[A:T, H:T], near2b[...])

        cut(full, i, 1, keep, send)


def gram(kernel, halves, tiles, later=(), weight=1):
    out = jax.ShapeDtypeStruct((4, halves * S, T), BF16)
    return pl.pallas_call(
        kernel,
        out_shape=(out, out),
        in_specs=[VMEM] * (len(tiles) + len(later)),
        out_specs=(VMEM, VMEM),
        scratch_shapes=[pltpu.VMEM((T, T), F32)],
        compiler_params=params(14),
        cost_estimate=cost(weight * halves * T * T * T, weight * 6 * T * T),
    )(*tiles, *later)


def local(kernel, shapes, *operands):
    out = tuple(jax.ShapeDtypeStruct(shape, BF16) for shape in shapes)
    return pl.pallas_call(
        kernel,
        out_shape=out,
        in_specs=[VMEM] * len(operands),
        out_specs=(VMEM,) * len(out),
        compiler_params=params(12),
        cost_estimate=cost(0, sum(4 * math.prod(shape) for shape in shapes)),
    )(*operands)


def rows_of(value, first, count, *later):
    def kernel(src, *refs):
        refs[-1][...] = src[first : first + count]

    return local(kernel, [(count,) + value.shape[1:]], value, *later)[0]


def gate(value, *later):
    return pl.pallas_call(
        lambda *refs: None,
        out_shape=jax.ShapeDtypeStruct(value.shape, value.dtype),
        in_specs=[VMEM] * (1 + len(later)),
        out_specs=VMEM,
        input_output_aliases={0: 0},
        compiler_params=params(8),
        cost_estimate=cost(0, 0),
    )(value, *later)


def add(*values):
    total = values[0].astype(F32)
    for value in values[1:]:
        total += value.astype(F32)
    return total


def sum_z_in_steps(keep, send):
    other = swap("core")(send)
    count = keep.shape[1]
    n = count // 32 * 16

    def step1(keep, other, by_up, by_down):
        by_up[...] = add(keep[2, 0:n], other[2, 0:n]).astype(BF16)
        by_down[...] = add(keep[2, n:count], other[2, n:count]).astype(BF16)

    def step2(keep, other, from_down, from_up, up, down):
        up[0:n] = add(keep[1, 0:n], other[1, 0:n], from_down[...]).astype(BF16)
        up[n:count] = add(keep[1, n:count], other[1, n:count]).astype(BF16)
        down[0:n] = add(keep[3, 0:n], other[3, 0:n]).astype(BF16)
        down[n:count] = add(keep[3, n:count], other[3, n:count], from_up[...]).astype(BF16)

    def step3(keep, other, from_down, from_up, out):
        out[...] = add(keep[0], other[0], from_down[...], from_up[...]).astype(BF16)

    up, down = local(step1, [(n, T), (count - n, T)], keep, other)
    up, down = ring("z", 1)(up), ring("z", -1)(down)
    up, down = local(step2, [(count, T)] * 2, keep, other, up, down)
    up, down = ring("z", 1)(up), ring("z", -1)(down)
    return local(step3, [(count, T)], keep, other, up, down)[0]


def sum_z(*pieces):
    pairs = [a for keep, send, _ in pieces for a in (keep, swap("core")(send))]
    moves = [(2 * i, *move) for i, piece in enumerate(pieces) for move in piece[2]]
    count = len(pairs)
    shape = (sum(move[2] for move in moves), T)

    def step1(*refs):
        for i, first, size, to in moves:
            rows = slice(first, first + size)
            for j, part in enumerate(refs[count:]):
                part[to : to + size] = add(refs[i][j + 1, rows], refs[i + 1][j + 1, rows]).astype(BF16)

    def step2(*refs):
        one, three, two, out = refs[count:]
        for i, first, size, to in moves:
            rows, at = slice(first, first + size), slice(to, to + size)
            out[at] = add(refs[i][0, rows], refs[i + 1][0, rows], one[at], three[at], two[at]).astype(BF16)

    parts = local(step1, [shape] * 3, *pairs)
    got = [ring("z", j)(parts[j - 1]) for j in (1, 3, 2)]
    return local(step2, [shape], *pairs, *got)[0]


def line_kernel(shard0, shard1, from_x1, shard2, from_x2, from_y, out):
    out[0 : 2 * S] = shard0[...]
    out[2 * S : 4 * S] = shard1[0 : 2 * S]
    out[4 * S : 6 * S] = from_y[0 : 2 * S]
    out[6 * S : 10 * S] = from_x1[...]
    high = (lax.axis_index("x") >= 2).astype(jnp.int32)
    for at, swapped, mine, theirs in (
        (10, lax.axis_index("yh"), shard1[4 * S : 5 * S], from_y[2 * S : 3 * S]),
        (12, high, shard2[0:S], from_x2[0:S]),
        (14, high, from_y[3 * S : 4 * S], from_x2[S : 2 * S]),
    ):
        out[pl.ds(pl.multiple_of((at + swapped) * S, S), S)] = mine
        out[pl.ds(pl.multiple_of((at + 1 - swapped) * S, S), S)] = theirs


RANGES = ((0, 0, 16), (1, 0, 16), (3, 0, 16), (2, 0, 8), (2, 8, 8))


TILES = (
    ((0, 0), "no"),
    ((1, 0), "no"),
    ((1, 1), "no"),
    ((3, 0), "yes"),
    ((3, 1), "yes"),
    ((0, 1), "h"),
    ((2, 0), "x"),
    ((2, 1), "x"),
)


def product_kernel(own, near1, far1, near3, far3, far, near2a, near2b, far2, *refs):
    x, h, z, k = (lax.axis_index(axis) for axis in ("x", "yh", "z", "core"))
    slices, (out_far, gram_far, g, g_sem, acc, out, gram_out, sems) = refs[:10], refs[10:]

    g_copies = []
    for c in range(2):
        for j, start, size in RANGES:
            core = k if c == 0 else 1 - k
            at = pl.multiple_of(core * (4 * S) + lax.rem(z + j, 4) * S, 16)
            n = len(g_copies)
            g_copies.append(pltpu.make_async_copy(slices[n], g.at[pl.ds(start, size), pl.ds(at, S)], g_sem.at[n]))
    for copy in g_copies:
        copy.start()
    for copy in g_copies:
        copy.wait()

    def tiles(first, count):
        return g[2 * first : 2 * (first + count)].reshape(count * T, T)

    def beside(parts):
        return jnp.concatenate(parts, axis=1)

    def either(turned, straight_way, turned_way):
        pl.when(jnp.logical_not(turned))(straight_way)
        pl.when(turned)(turned_way)

    line = lax.axis_index("yl") * 4 + z
    dx, dh = lax.rem(line // 2 - x + 4, 4), lax.rem(line + h, 2)
    for t, ((ax, ah), turn) in enumerate(TILES):
        mine, turned = (dx == ax) & (dh == ah), {"no": z < 0, "yes": z >= 0, "h": h != 0, "x": x >= 2}[turn]
        if turn != "yes":

            @pl.when(mine & jnp.logical_not(turned))
            def _():
                gram_out[...] = g[2 * t + k]

        if turn != "no":
            for side in range(2):

                @pl.when(mine & turned & (k == side))
                def _():
                    gram_out[...] = g[2 * t : 2 * t + 2, :, side * H : (side + 1) * H].reshape(T, H).T

    copies = [pltpu.make_async_copy(gram_out, gram_far, sems.at[2])]
    for i in range(2):
        rows = pl.ds(i * H, H)
        copies.append(pltpu.make_async_copy(out.at[rows], out_far.at[rows], sems.at[i]))
    copies[0].start()

    def far_straight():
        acc[...] = dot(far[...], tiles(5, 1))

    def far_turned():
        acc[...] = dot_t(far[...], tiles(5, 1))

    either(h != 0, far_straight, far_turned)
    acc[...] += dot(beside([own[...], near1[...], far1[...]]), tiles(0, 3))
    acc[...] += dot_t(beside([near3[...], far3[...]]), beside([tiles(3, 1), tiles(4, 1)]))

    def finish(multiply, factor):
        for i, near2 in enumerate((near2a, near2b)):
            rows = slice(i * H, (i + 1) * H)
            total = acc[rows, :] + multiply(beside([near2[...], far2[rows, :]]), factor)
            out[rows, :] = (1.5 * own[rows, :].astype(F32) - 0.5 * total).astype(BF16)
            copies[1 + i].start()

    either(
        x >= 2,
        lambda: finish(dot, tiles(6, 2)),
        lambda: finish(dot_t, beside([tiles(6, 1), tiles(7, 1)])),
    )
    for copy in copies:
        copy.wait()


def product(tiles, slices):
    operands = [*tiles, *slices]
    return pl.pallas_call(
        product_kernel,
        out_shape=(jax.ShapeDtypeStruct((T, T), BF16), jax.ShapeDtypeStruct((H, T), BF16)),
        in_specs=[VMEM] * len(operands),
        out_specs=(ANY, ANY),
        scratch_shapes=[
            pltpu.VMEM((16, H, T), BF16),
            pltpu.SemaphoreType.DMA((len(slices),)),
            pltpu.VMEM((T, T), F32),
            pltpu.VMEM((T, T), BF16),
            pltpu.VMEM((H, T), BF16),
            pltpu.SemaphoreType.DMA((3,)),
        ],
        compiler_params=params(30),
        cost_estimate=cost(16 * T * T * T, 36 * T * T),
    )(*operands)


def sum_yl(total):
    total = total.astype(F32) + swap("yl")(total).astype(F32)
    return (total * (1.0 / N)).astype(BF16)


def body(quant_codes, block_scales):
    own = dequant(quant_codes, block_scales)

    near1 = ring("x", -1)(own)
    near3 = ring("x", 1)(own)
    far = swap("yh")(own)
    total0 = sum_z_in_steps(*gram(gram_kernel0, 2, [own]))
    down, up = rows_of(near1, 0, H, total0, far), rows_of(near3, H, H, total0, far)
    near2 = (ring("x", -1)(down), ring("x", 1)(up))

    piece1a = gram(gram_kernel1a, 3, [own, near1, far], [total0, down, up])
    piece1b = gram(gram_kernel1b, 2, [near1, far], [piece1a[0]], 0)
    total1 = sum_z((*piece1a, ((0, 2 * S, 0), (2 * S, S, 4 * S))), (*piece1b, ((0, 2 * S, 2 * S),)))
    total2 = sum_z((*gram(gram_kernel2, 2, [own, far, *near2], [total1]), ((0, 2 * S, 0),)))
    shard0, shard1, shard2 = sum_yl(total0), sum_yl(total1), sum_yl(total2)
    from_x1 = ring("x", 1)(shard1[: 4 * S])
    from_x2 = ring("x", 2)(shard2)

    def to_y(first, second, out):
        out[0 : 3 * S] = first[2 * S : 5 * S]
        out[3 * S : 4 * S] = second[S : 2 * S]

    from_y = swap("yh")(local(to_y, [(4 * S, T)], shard1, shard2)[0])
    line = local(line_kernel, [(16 * S, T)], shard0, shard1, from_x1, shard2, from_x2, from_y)[0]

    def stack(top, bottom, _, out):
        out[0:H] = top[...]
        out[H:T] = bottom[...]

    again = rows_of(far, 0, T, line)
    far1, far3 = ring("x", -1)(again), ring("x", 1)(again)
    far2 = swap("yh")(local(stack, [(T, T)], *near2, line)[0])
    line = line.reshape(16, S, T)
    one, three = ring("z", -1)(line), ring("z", 1)(line)
    two = [ring("z", -1)(rows_of(one, 0, 8)), ring("z", 1)(rows_of(three, 8, 8))]
    two = [gate(a, far1, far2, far3) for a in two]
    mine = [line, one, three, *two]
    slices = mine + [swap("core")(a) for a in mine]
    return product([own, near1, far1, near3, far3, far, *near2, far2], slices)


def solution(mesh):
    split = Mesh(mesh.devices.reshape(2, 4, 4, 2, 2), AXES)
    line, side = ("yl", "z", "core"), ("x", "yh")
    return jax.shard_map(
        body,
        mesh=split,
        in_specs=(P(line, side), P(side, line)),
        out_specs=(P(line, side), P(line, side)),
        check_vma=False,
    )
```

```python
import math

import jax
import jax.numpy as jnp
from jax import lax
from jax.experimental import pallas as pl
from jax.experimental.pallas import tpu as pltpu
from jax.sharding import Mesh, PartitionSpec as P

N = 12288
BLOCK = 64
AXES = ("yl", "z", "x", "yh", "core")
F32, BF16 = jnp.float32, jnp.bfloat16
T = 768
H = T // 2
A = H
S = 48
VMEM = pl.BlockSpec(memory_space=pltpu.VMEM)
ANY = pl.BlockSpec(memory_space=pl.ANY)


def ring(axis, step):
    return lambda a: lax.ppermute(a, axis, [(i, (i + step) % 4) for i in range(4)])


def swap(axis):
    return lambda a: lax.ppermute(a, axis, [(0, 1), (1, 0)])


def across(axis, step, other):
    first, axes = AXES.index(axis) < AXES.index(other), sorted((axis, other), key=AXES.index)
    count = 4 if axis in "xz" else 2
    at = (lambda i, o: i * 2 + o) if first else (lambda i, o: o * count + i)
    moves = [(at(i, o), at((i + step) % count, 1 - o)) for i in range(count) for o in range(2)]
    return lambda a: lax.ppermute(a, tuple(axes), moves)


def tdot(a, b):
    return lax.dot_general(a, b, (((0,), (0,)), ((), ())), preferred_element_type=F32)


def dot(a, b):
    return jnp.dot(a, b, preferred_element_type=F32)


def dot_t(a, b):
    return lax.dot_general(a, b, (((1,), (1,)), ((), ())), preferred_element_type=F32)


def params(mib):
    return pltpu.CompilerParams(vmem_limit_bytes=mib << 20)


def cost(flops, size):
    return pl.CostEstimate(flops=flops, bytes_accessed=size, transcendentals=0)


def dequant_kernel(codes, scales, out):
    factor = scales[...].T
    lane = lax.broadcasted_iota(jnp.int32, (T, 128), 1)
    for g in range(T // 128):
        both = jnp.where(lane < BLOCK, factor[:, 2 * g : 2 * g + 1], factor[:, 2 * g + 1 : 2 * g + 2])
        levels = codes[:, 128 * g : 128 * (g + 1)].astype(F32) - 7.5
        out[:, 128 * g : 128 * (g + 1)] = (levels * both).astype(BF16)


def dequant(codes, scales):
    return pl.pallas_call(
        dequant_kernel,
        out_shape=jax.ShapeDtypeStruct((T, T), BF16),
        in_specs=[VMEM, VMEM],
        out_specs=VMEM,
        compiler_params=params(12),
        cost_estimate=cost(2 * T * T, 6 * T * T),
    )(codes, scales)


def cut(full, first, count, keep, send):
    z, k = lax.axis_index("z"), lax.axis_index("core")
    for half in range(count):
        for j in range(4):
            at = half * H + lax.rem(z + j, 4) * S
            to = pl.ds((first + half) * S, S)
            keep[j, to, :] = full[pl.ds(pl.multiple_of(at + k * (4 * S), 16), S), :].astype(BF16)
            send[j, to, :] = full[pl.ds(pl.multiple_of(at + (1 - k) * (4 * S), 16), S), :].astype(BF16)


def gram_kernel0(own, keep, send, full):
    full[...] = tdot(own[...], own[...])
    cut(full, 0, 2, keep, send)


def gram_kernel1a(own, near1, far, _, __, ___, keep, send, full):
    full[...] = tdot(near1[...], own[...])
    cut(full, 0, 2, keep, send)
    h = lax.axis_index("yh")

    @pl.when(h == 0)
    def _():
        full[0:H, :] = tdot(far[:, 0:H], own[...])

    @pl.when(h != 0)
    def _():
        full[0:H, :] = tdot(own[:, H:T], far[...])

    cut(full, 2, 1, keep, send)


def gram_kernel1b(near1, far, _, keep, send, full):
    full[...] = tdot(near1[...], far[...])
    cut(full, 0, 2, keep, send)


def gram_kernel2(own, far, near2a, near2b, _, keep, send, full):
    low = lax.axis_index("x") < 2
    for i, other in enumerate((own, far)):

        @pl.when(low)
        def _():
            full[0:H, :] = tdot(near2a[:, 0:H], other[0:A, :]) + tdot(near2b[:, 0:H], other[A:T, :])

        @pl.when(jnp.logical_not(low))
        def _():
            full[0:H, :] = tdot(other[0:A, H:T], near2a[...]) + tdot(other[A:T, H:T], near2b[...])

        cut(full, i, 1, keep, send)


def gram(kernel, halves, tiles, later=(), weight=1):
    out = jax.ShapeDtypeStruct((4, halves * S, T), BF16)
    return pl.pallas_call(
        kernel,
        out_shape=(out, out),
        in_specs=[VMEM] * (len(tiles) + len(later)),
        out_specs=(VMEM, VMEM),
        scratch_shapes=[pltpu.VMEM((T, T), F32)],
        compiler_params=params(14),
        cost_estimate=cost(weight * halves * T * T * T, weight * 6 * T * T),
    )(*tiles, *later)


def local(kernel, shapes, *operands):
    out = tuple(jax.ShapeDtypeStruct(shape, BF16) for shape in shapes)
    return pl.pallas_call(
        kernel,
        out_shape=out,
        in_specs=[VMEM] * len(operands),
        out_specs=(VMEM,) * len(out),
        compiler_params=params(12),
        cost_estimate=cost(0, sum(4 * math.prod(shape) for shape in shapes)),
    )(*operands)


def rows_of(value, first, count, *later):
    def kernel(src, *refs):
        refs[-1][...] = src[first : first + count]

    return local(kernel, [(count,) + value.shape[1:]], value, *later)[0]


def gate(value, *later):
    return pl.pallas_call(
        lambda *refs: None,
        out_shape=jax.ShapeDtypeStruct(value.shape, value.dtype),
        in_specs=[VMEM] * (1 + len(later)),
        out_specs=VMEM,
        input_output_aliases={0: 0},
        compiler_params=params(8),
        cost_estimate=cost(0, 0),
    )(value, *later)


def add(*values):
    total = values[0].astype(F32)
    for value in values[1:]:
        total += value.astype(F32)
    return total


def sum_z_in_steps(keep, send):
    other = swap("core")(send)
    count = keep.shape[1]
    n = count // 32 * 16

    def step1(keep, other, by_up, by_down):
        by_up[...] = add(keep[2, 0:n], other[2, 0:n]).astype(BF16)
        by_down[...] = add(keep[2, n:count], other[2, n:count]).astype(BF16)

    def step2(keep, other, from_down, from_up, up, down):
        up[0:n] = add(keep[1, 0:n], other[1, 0:n], from_down[...]).astype(BF16)
        up[n:count] = add(keep[1, n:count], other[1, n:count]).astype(BF16)
        down[0:n] = add(keep[3, 0:n], other[3, 0:n]).astype(BF16)
        down[n:count] = add(keep[3, n:count], other[3, n:count], from_up[...]).astype(BF16)

    def step3(keep, other, from_down, from_up, out):
        out[...] = add(keep[0], other[0], from_down[...], from_up[...]).astype(BF16)

    up, down = local(step1, [(n, T), (count - n, T)], keep, other)
    up, down = ring("z", 1)(up), ring("z", -1)(down)
    up, down = local(step2, [(count, T)] * 2, keep, other, up, down)
    up, down = ring("z", 1)(up), ring("z", -1)(down)
    return local(step3, [(count, T)], keep, other, up, down)[0]


def sum_z(*pieces):
    pairs = [a for keep, send, _ in pieces for a in (keep, swap("core")(send))]
    moves = [(2 * i, *move) for i, piece in enumerate(pieces) for move in piece[2]]
    count = len(pairs)
    shape = (sum(move[2] for move in moves), T)

    def step1(*refs):
        for i, first, size, to in moves:
            rows = slice(first, first + size)
            for j, part in enumerate(refs[count:]):
                part[to : to + size] = add(refs[i][j + 1, rows], refs[i + 1][j + 1, rows]).astype(BF16)

    def step2(*refs):
        one, three, two, out = refs[count:]
        for i, first, size, to in moves:
            rows, at = slice(first, first + size), slice(to, to + size)
            out[at] = add(refs[i][0, rows], refs[i + 1][0, rows], one[at], three[at], two[at]).astype(BF16)

    parts = local(step1, [shape] * 3, *pairs)
    got = [ring("z", j)(parts[j - 1]) for j in (1, 3, 2)]
    return local(step2, [shape], *pairs, *got)[0]


def line_kernel(shard0, shard1, from_x1, shard2, from_x2, from_y, out):
    out[0 : 2 * S] = shard0[...]
    out[2 * S : 4 * S] = shard1[0 : 2 * S]
    out[4 * S : 6 * S] = from_y[0 : 2 * S]
    out[6 * S : 10 * S] = from_x1[...]
    high = (lax.axis_index("x") >= 2).astype(jnp.int32)
    for at, swapped, mine, theirs in (
        (10, lax.axis_index("yh"), shard1[4 * S : 5 * S], from_y[2 * S : 3 * S]),
        (12, high, shard2[0:S], from_x2[0:S]),
        (14, high, from_y[3 * S : 4 * S], from_x2[S : 2 * S]),
    ):
        out[pl.ds(pl.multiple_of((at + swapped) * S, S), S)] = mine
        out[pl.ds(pl.multiple_of((at + 1 - swapped) * S, S), S)] = theirs


RANGES = ((0, 0, 16), (1, 0, 16), (3, 0, 16), (2, 0, 8), (2, 8, 8))


TILES = (
    ((0, 0), "no"),
    ((1, 0), "no"),
    ((1, 1), "no"),
    ((3, 0), "yes"),
    ((3, 1), "yes"),
    ((0, 1), "h"),
    ((2, 0), "x"),
    ((2, 1), "x"),
)


def product_kernel(own, near1, far1, near3, far3, far, near2a, near2b, far2, *refs):
    x, h, z, k = (lax.axis_index(axis) for axis in ("x", "yh", "z", "core"))
    slices, (out_far, gram_far, g, g_sem, acc, out, gram_out, sems) = refs[:10], refs[10:]

    g_copies = []
    for c in range(2):
        for j, start, size in RANGES:
            core = k if c == 0 else 1 - k
            at = pl.multiple_of(core * (4 * S) + lax.rem(z + j, 4) * S, 16)
            n = len(g_copies)
            g_copies.append(pltpu.make_async_copy(slices[n], g.at[pl.ds(start, size), pl.ds(at, S)], g_sem.at[n]))
    for copy in g_copies:
        copy.start()
    for copy in g_copies:
        copy.wait()

    def tiles(first, count):
        return g[2 * first : 2 * (first + count)].reshape(count * T, T)

    def beside(parts):
        return jnp.concatenate(parts, axis=1)

    def either(turned, straight_way, turned_way):
        pl.when(jnp.logical_not(turned))(straight_way)
        pl.when(turned)(turned_way)

    line = lax.axis_index("yl") * 4 + z
    dx, dh = lax.rem(line // 2 - x + 4, 4), lax.rem(line + h, 2)
    for t, ((ax, ah), turn) in enumerate(TILES):
        mine, turned = (dx == ax) & (dh == ah), {"no": z < 0, "yes": z >= 0, "h": h != 0, "x": x >= 2}[turn]
        if turn != "yes":

            @pl.when(mine & jnp.logical_not(turned))
            def _():
                gram_out[...] = g[2 * t + k]

        if turn != "no":
            for side in range(2):

                @pl.when(mine & turned & (k == side))
                def _():
                    gram_out[...] = g[2 * t : 2 * t + 2, :, side * H : (side + 1) * H].reshape(T, H).T

    copies = [pltpu.make_async_copy(gram_out, gram_far, sems.at[2])]
    for i in range(2):
        rows = pl.ds(i * H, H)
        copies.append(pltpu.make_async_copy(out.at[rows], out_far.at[rows], sems.at[i]))
    copies[0].start()

    def far_straight():
        acc[...] = dot(far[...], tiles(5, 1))

    def far_turned():
        acc[...] = dot_t(far[...], tiles(5, 1))

    either(h != 0, far_straight, far_turned)
    acc[...] += dot(beside([near1[...], far1[...]]), tiles(1, 2))
    acc[...] += dot_t(beside([own[...], near3[...], far3[...]]), beside([tiles(0, 1), tiles(3, 1), tiles(4, 1)]))

    def finish(multiply, factor):
        for i, near2 in enumerate((near2a, near2b)):
            rows = slice(i * H, (i + 1) * H)
            total = acc[rows, :] + multiply(beside([near2[...], far2[rows, :]]), factor)
            out[rows, :] = (1.5 * own[rows, :].astype(F32) - 0.5 * total).astype(BF16)
            copies[1 + i].start()

    either(
        x >= 2,
        lambda: finish(dot, tiles(6, 2)),
        lambda: finish(dot_t, beside([tiles(6, 1), tiles(7, 1)])),
    )
    for copy in copies:
        copy.wait()


def product(tiles, slices):
    operands = [*tiles, *slices]
    return pl.pallas_call(
        product_kernel,
        out_shape=(jax.ShapeDtypeStruct((T, T), BF16), jax.ShapeDtypeStruct((H, T), BF16)),
        in_specs=[VMEM] * len(operands),
        out_specs=(ANY, ANY),
        scratch_shapes=[
            pltpu.VMEM((16, H, T), BF16),
            pltpu.SemaphoreType.DMA((len(slices),)),
            pltpu.VMEM((T, T), F32),
            pltpu.VMEM((T, T), BF16),
            pltpu.VMEM((H, T), BF16),
            pltpu.SemaphoreType.DMA((3,)),
        ],
        compiler_params=params(30),
        cost_estimate=cost(16 * T * T * T, 36 * T * T),
    )(*operands)


def sum_yl(total):
    total = total.astype(F32) + swap("yl")(total).astype(F32)
    return (total * (1.0 / N)).astype(BF16)


def body(quant_codes, block_scales):
    own = dequant(quant_codes, block_scales)

    near1 = ring("x", -1)(own)
    near3 = ring("x", 1)(own)
    far = swap("yh")(own)
    total0 = sum_z_in_steps(*gram(gram_kernel0, 2, [own]))
    down, up = rows_of(near1, 0, H, total0, far), rows_of(near3, H, H, total0, far)
    near2 = (ring("x", -1)(down), ring("x", 1)(up))

    piece1a = gram(gram_kernel1a, 3, [own, near1, far], [total0, down, up])
    piece1b = gram(gram_kernel1b, 2, [near1, far], [piece1a[0]], 0)
    total1 = sum_z((*piece1a, ((0, 2 * S, 0), (2 * S, S, 4 * S))), (*piece1b, ((0, 2 * S, 2 * S),)))
    total2 = sum_z((*gram(gram_kernel2, 2, [own, far, *near2], [total1]), ((0, 2 * S, 0),)))
    shard0, shard1, shard2 = sum_yl(total0), sum_yl(total1), sum_yl(total2)
    from_x1 = ring("x", 1)(shard1[: 4 * S])
    from_x2 = ring("x", 2)(shard2)

    def to_y(first, second, out):
        out[0 : 3 * S] = first[2 * S : 5 * S]
        out[3 * S : 4 * S] = second[S : 2 * S]

    from_y = swap("yh")(local(to_y, [(4 * S, T)], shard1, shard2)[0])
    line = local(line_kernel, [(16 * S, T)], shard0, shard1, from_x1, shard2, from_x2, from_y)[0]

    def stack(top, bottom, _, out):
        out[0:H] = top[...]
        out[H:T] = bottom[...]

    again = rows_of(far, 0, T, line)
    far1, far3 = ring("x", -1)(again), ring("x", 1)(again)
    far2 = swap("yh")(local(stack, [(T, T)], *near2, line)[0])
    line = line.reshape(16, S, T)
    one, three = ring("z", -1)(line), ring("z", 1)(line)
    two = [ring("z", -1)(rows_of(one, 0, 8)), ring("z", 1)(rows_of(three, 8, 8))]
    two = [gate(a, far1, far2, far3) for a in two]
    mine = [line, one, three, *two]
    slices = mine + [swap("core")(a) for a in mine]
    return product([own, near1, far1, near3, far3, far, *near2, far2], slices)


def solution(mesh):
    split = Mesh(mesh.devices.reshape(2, 4, 4, 2, 2), AXES)
    line, side = ("yl", "z", "core"), ("x", "yh")
    return jax.shard_map(
        body,
        mesh=split,
        in_specs=(P(line, side), P(side, line)),
        out_specs=(P(line, side), P(line, side)),
        check_vma=False,
    )
```
